32 devices in a mesh: outer: 4 (over y, x), inner: 8 (over z, core).
Axes of the slice: x: 2, y: 2, z: 4, core: 2. Of those that a mesh axis runs over, the one named last changes fastest.
Arguments:
- query_rows: bfloat16 [4096, 4096], P(('outer', 'inner')), may hold values from -6 to 6
- key_rows: bfloat16 [4096, 4096], P(('outer', 'inner')), may hold values from -6 to 6
- value_rows: bfloat16 [4096, 4096], P(('outer', 'inner')), may hold values from -6 to 6
- out_grad: bfloat16 [4096, 4096], P(('outer', 'inner')), may hold values from -6 to 6
- filter_rows: bfloat16 [4096, 4096], P(('outer', 'inner')), may hold values from -0.09375 to 0.09375
- skip_gain: float32 [4096], replicated, may hold values from -1 to 1
Outputs:
- layer_out: bfloat16 [4096, 4096], P(('outer', 'inner'))
- query_grad: bfloat16 [4096, 4096], P(('outer', 'inner'))
- key_grad: bfloat16 [4096, 4096], P(('outer', 'inner'))
- value_grad: bfloat16 [4096, 4096], P(('outer', 'inner'))
- filter_grad: bfloat16 [4096, 4096], P(('outer', 'inner'))
- skip_grad: float32 [4096], replicated
The draws below stay inside these ranges and needn't reach their ends.
All inputs are finite; a program needn't handle non-finite values.
Results may differ from the reference program's by a relative error of at most 0.0085.
Values may be sent and summed in bfloat16 or wider, within the bound.
No kernel may reach another device: no remote copies, remote signals or barrier semaphores. Data moves between devices by JAX's collectives and lax.ppermute only.
A program may use at most 128 MiB of HBM per device.

```python
import math
import jax
import jax.numpy as jnp
from jax import lax

CHANNELS = 4096
TOK_DEV = 128
TOKENS = 4096
N_OUTER = 4
N_INNER = 8


def steps_of(rng, shape, cuts, smallest, largest):
    def one(dim, blocks):
        heights = jax.random.uniform(jax.random.fold_in(jax.random.fold_in(rng, 6), dim), (blocks,), jnp.float32, smallest / len(cuts), largest / len(cuts))
        return jnp.repeat(jnp.exp(heights), shape[dim] // blocks).reshape((-1,) + (1,) * (len(shape) - dim - 1))

    loudness = one(*cuts[0])
    for cut in cuts[1:]:
        loudness = loudness * one(*cut)
    return loudness


def noise(stream_key, dims, scale, limit, shards=(), held_as=jnp.bfloat16):
    factor_of = steps_of(stream_key, dims, shards, -0.22, 0.18) if shards else 1.0
    values = jax.random.normal(stream_key, dims, jnp.float32) * scale * factor_of
    return jnp.minimum(jnp.maximum(values, -limit), limit).astype(held_as)


def setup_inputs(seed: int = 0) -> dict:
    keys = jax.random.split(jax.random.key(seed), 7)
    return {
        "query_rows": noise(keys[0], (TOKENS, CHANNELS), 1.0, 6.0, ((0, 32),)),
        "key_rows": noise(keys[1], (TOKENS, CHANNELS), 1.0, 6.0, ((0, 32),)),
        "value_rows": noise(keys[2], (TOKENS, CHANNELS), 1.0, 6.0, ((0, 32),)),
        "out_grad": noise(keys[3], (TOKENS, CHANNELS), 1.0, 6.0, ((0, 32),)),
        "filter_rows": noise(keys[4], (TOKENS, CHANNELS), TOKENS ** -0.5, 0.09375, ((0, 32),)),
        "skip_gain": jnp.clip(jax.random.uniform(keys[5], (CHANNELS,), jnp.float32, -1.0, 1.0), -1.0, 1.0),
    }


TWO_PI = 2.0 * math.pi
HIGH = lax.Precision.HIGHEST

def settle(values):
    rounded = values.astype(jnp.bfloat16)
    return lax.optimization_barrier(rounded).astype(jnp.float32)

def rounded_trig(phase, modulus):
    angle = (phase % modulus).astype(jnp.float32) * (TWO_PI / modulus)
    return (settle(jnp.cos(angle)), settle(jnp.sin(angle)))

def make_tables():
    devices = N_OUTER * N_INNER
    radix_count = 2 * devices
    points = 2 * TOKENS
    rows = jnp.arange(devices, dtype=jnp.int32)
    freqs = jnp.arange(radix_count, dtype=jnp.int32)
    steps = jnp.arange(TOK_DEV, dtype=jnp.int32)
    first_phase = rows[None, None, :] * freqs[None, :, None] * TOK_DEV + steps[:, None, None] * freqs[None, :, None]
    first = rounded_trig(first_phase, points)
    second = rounded_trig(steps[:, None] * steps[None, :], TOK_DEV)
    third_phase = steps[None, :, None] * steps[None, None, :] * radix_count + steps[None, :, None] * freqs[:, None, None]
    third = rounded_trig(third_phase, points)
    last = rounded_trig(rows[:, None] * freqs[None, :], radix_count)
    return (first, second, third, last)

def spectrum_of(signal, tables):
    devices = N_OUTER * N_INNER
    (first_cos, first_sin), (step_cos, step_sin) = (tables[0], tables[1])
    width = signal.shape[1]
    grid = signal.astype(jnp.float32).reshape(devices, TOK_DEV, width)
    one_real = settle(jnp.einsum('skr,rsc->ksc', first_cos, grid, precision=HIGH))
    one_imag = settle(-jnp.einsum('skr,rsc->ksc', first_sin, grid, precision=HIGH))
    spec_real = jnp.einsum('ksc,sq->kqc', one_real, step_cos, precision=HIGH) + jnp.einsum('ksc,sq->kqc', one_imag, step_sin, precision=HIGH)
    spec_imag = jnp.einsum('ksc,sq->kqc', one_imag, step_cos, precision=HIGH) - jnp.einsum('ksc,sq->kqc', one_real, step_sin, precision=HIGH)
    return (spec_real, spec_imag)

def inverse_of(q_real, q_imag, tables):
    devices = N_OUTER * N_INNER
    points = 2 * TOKENS
    (third_cos, third_sin), (last_cos, last_sin) = (tables[2], tables[3])
    q_real = settle(q_real)
    q_imag = settle(q_imag)
    three_real = settle(jnp.einsum('kqc,ksq->ksc', q_real, third_cos, precision=HIGH) - jnp.einsum('kqc,ksq->ksc', q_imag, third_sin, precision=HIGH))
    three_imag = settle(jnp.einsum('kqc,ksq->ksc', q_real, third_sin, precision=HIGH) + jnp.einsum('kqc,ksq->ksc', q_imag, third_cos, precision=HIGH))
    values = (jnp.einsum('rk,ksc->rsc', last_cos, three_real, precision=HIGH) - jnp.einsum('rk,ksc->rsc', last_sin, three_imag, precision=HIGH)) / points
    return values.reshape(devices * TOK_DEV, values.shape[2]).astype(jnp.bfloat16)

def reference(query_rows, key_rows, value_rows, out_grad, filter_rows, skip_gain):
    factor = 1.0 / math.sqrt(TOKENS)
    product = (key_rows.astype(jnp.float32) * value_rows.astype(jnp.float32)).astype(jnp.bfloat16)
    gate_grad = out_grad.astype(jnp.float32) * query_rows.astype(jnp.float32)
    gate_half = gate_grad.astype(jnp.bfloat16)
    tables = make_tables()
    block = math.gcd(CHANNELS, 256)
    count = CHANNELS // block

    def per_block(index):
        start = (index * block).astype(jnp.int32)
        product_block = lax.dynamic_slice_in_dim(product, start, block, 1)
        gate_block = lax.dynamic_slice_in_dim(gate_half, start, block, 1)
        filter_block = lax.dynamic_slice_in_dim(filter_rows, start, block, 1)
        value_real, value_imag = spectrum_of(product_block, tables)
        gate_real, gate_imag = spectrum_of(gate_block, tables)
        filter_real, filter_imag = spectrum_of(filter_block, tables)
        convolved = inverse_of(value_real * filter_real - value_imag * filter_imag, value_real * filter_imag + value_imag * filter_real, tables)
        correlated = inverse_of(filter_real * gate_real + filter_imag * gate_imag, filter_real * gate_imag - filter_imag * gate_real, tables)
        lagged = inverse_of((value_real * gate_real + value_imag * gate_imag) * factor, (value_real * gate_imag - value_imag * gate_real) * factor, tables)
        return (convolved, correlated, lagged)
    convolved, correlated, lagged = lax.map(per_block, jnp.arange(count, dtype=jnp.int32))
    convolved = convolved.transpose(1, 0, 2).reshape(TOKENS, CHANNELS).astype(jnp.float32)
    correlated = correlated.transpose(1, 0, 2).reshape(TOKENS, CHANNELS).astype(jnp.float32)
    filter_grad = lagged.transpose(1, 0, 2).reshape(TOKENS, CHANNELS)
    product_full = product.astype(jnp.float32)
    mixing = convolved + skip_gain[None, :] * product_full
    layer_out = (query_rows.astype(jnp.float32) * mixing).astype(jnp.bfloat16)
    query_grad = (out_grad.astype(jnp.float32) * mixing).astype(jnp.bfloat16)
    carried = correlated + skip_gain[None, :] * gate_grad
    key_grad = (carried * value_rows.astype(jnp.float32)).astype(jnp.bfloat16)
    value_grad = (carried * key_rows.astype(jnp.float32)).astype(jnp.bfloat16)
    skip_grad = lax.optimization_barrier(jnp.sum(gate_grad * product_full, axis=0)) * factor
    return (layer_out, query_grad, key_grad, value_grad, filter_grad, skip_grad)
```

```python
import functools
import math

import jax
import jax.numpy as jnp
import ml_dtypes
import numpy as np
from jax import lax
from jax.experimental import pallas as pl
from jax.experimental.pallas import tpu as pltpu
from jax.sharding import PartitionSpec as P

TWO_PI = 2.0 * math.pi
AXES = ("outer", "inner")
LANES = 128
SUBLANES = 8
BF16 = jnp.bfloat16
F32 = jnp.float32


def table_trig(phase, modulus):
    angle = (phase % modulus).astype(np.float32) * np.float32(TWO_PI / modulus)
    return tuple(
        part.astype(ml_dtypes.bfloat16).astype(np.float32) for part in (np.cos(angle), np.sin(angle))
    )


def make_tables(rows, steps):
    planes = rows + 1
    points = 2 * rows * steps
    row = np.arange(rows)
    plane = np.arange(planes)
    step = np.arange(steps)
    eye = np.eye(SUBLANES, dtype=np.float32)
    phase = row[None, None, :] * plane[None, :, None] * steps + step[:, None, None] * plane[None, :, None]
    cos, sin = table_trig(phase, points)
    first = np.stack([cos, -sin], axis=1).reshape(steps // SUBLANES, SUBLANES, 2, planes, rows)
    first = np.einsum("bipkr,ij->bpkirj", first, eye)
    first = first.reshape(steps // SUBLANES, 2 * planes * SUBLANES, rows * SUBLANES)
    cos, sin = table_trig(step[:, None] * step[None, :], steps)
    second = np.block([[cos, sin], [-sin, cos]])
    phase = step[None, :, None] * step[None, None, :] * (2 * rows) + step[None, :, None] * plane[:, None, None]
    cos, sin = table_trig(phase, points)
    third = np.concatenate(
        [np.concatenate([cos, -sin], axis=2), np.concatenate([sin, cos], axis=2)], axis=1
    )
    cos, sin = table_trig(row[:, None] * plane[None, :], 2 * rows)
    weight = np.where((plane == 0) | (plane == rows), 1.0, 2.0).astype(np.float32)
    last = np.stack([cos * weight, -sin * weight], axis=1)
    last = np.einsum("rpk,ij->ripkj", last, eye).reshape(rows * SUBLANES, 2 * planes * SUBLANES)
    return tuple(table.astype(ml_dtypes.bfloat16) for table in (first, second, third, last))


def dot(a, b):
    return jnp.dot(a, b, preferred_element_type=F32)


def pack_kernel(filter_ref, key_ref, value_ref, out_ref):
    blocks = out_ref.shape[0]
    tokens = filter_ref.shape[0]
    for j in range(blocks):
        cols = pl.ds(j * LANES, LANES)
        out_ref[j, :tokens, :] = filter_ref[:, cols]
        product = key_ref[:, cols].astype(F32) * value_ref[:, cols].astype(F32)
        out_ref[j, tokens:, :] = product.astype(BF16)


def gate_kernel(query_ref, grad_ref, key_ref, value_ref, out_ref, skip_ref):
    blocks = out_ref.shape[0]
    for j in range(blocks):
        cols = pl.ds(j * LANES, LANES)
        gate = grad_ref[:, cols].astype(F32) * query_ref[:, cols].astype(F32)
        product = (key_ref[:, cols].astype(F32) * value_ref[:, cols].astype(F32)).astype(BF16).astype(F32)
        out_ref[j] = gate.astype(BF16)
        skip_ref[:, cols] = jnp.sum(gate * product, axis=0, keepdims=True)


def spectra_of(read_pair, first_ref, second_ref, section, store):
    planes = section.shape[0]
    steps = section.shape[1] // 2
    width = section.shape[2]

    def one(b, _):
        pair = read_pair(b)
        for half in range(2):
            block = pair[:, half * SUBLANES : (half + 1) * SUBLANES, :]
            flat = block.reshape(-1, width).astype(BF16)
            result = dot(first_ref[2 * b + half], flat).reshape(2, planes, SUBLANES, width)
            at = pl.multiple_of((2 * b + half) * SUBLANES, SUBLANES)
            section[:, pl.ds(at, SUBLANES), :] = result[0]
            section[:, pl.ds(steps + at, SUBLANES), :] = result[1]
        return 0

    lax.fori_loop(0, steps // (2 * SUBLANES), one, 0)

    def two(k, _):
        store(k, dot(second_ref[...], section[k].astype(BF16)))
        return 0

    lax.fori_loop(0, planes, two, 0)


def inverse_of(product_at, third_ref, last_ref, section, scale, write_pair):
    planes = section.shape[0]
    steps = section.shape[1] // 2
    width = section.shape[2]

    def three(k, _):
        section[k] = dot(third_ref[k], product_at(k))
        return 0

    lax.fori_loop(0, planes, three, 0)

    def four(b, _):
        halves = []
        for half in range(2):
            at = pl.multiple_of((2 * b + half) * SUBLANES, SUBLANES)
            real = section[:, pl.ds(at, SUBLANES), :].reshape(-1, width)
            imag = section[:, pl.ds(steps + at, SUBLANES), :].reshape(-1, width)
            flat = jnp.concatenate([real, imag], axis=0).astype(BF16)
            halves.append((dot(last_ref[...], flat) * scale).reshape(-1, SUBLANES, width))
        write_pair(b, jnp.concatenate(halves, axis=1))
        return 0

    lax.fori_loop(0, steps // (2 * SUBLANES), four, 0)


def pair_rows(b):
    return pl.ds(pl.multiple_of(b * 2 * SUBLANES, 2 * SUBLANES), 2 * SUBLANES)


def forward_kernel(steps, scale, packed_ref, first_ref, second_ref, third_ref, last_ref, out_ref, spectra_ref, section, narrow):
    def read_pair(b):
        return jnp.concatenate(
            [
                packed_ref[:, pair_rows(b), :].astype(F32),
                packed_ref[:, pair_rows(b + steps // (2 * SUBLANES)), :].astype(F32),
            ],
            axis=2,
        )

    def store(k, plane):
        spectra_ref[k] = plane

    spectra_of(read_pair, first_ref, second_ref, section, store)

    def product_at(k):
        filt = spectra_ref[k, :, :LANES]
        value = spectra_ref[k, :, LANES:]
        fr, fi, vr, vi = filt[:steps], filt[steps:], value[:steps], value[steps:]
        return jnp.concatenate([vr * fr - vi * fi, vr * fi + vi * fr], axis=0).astype(BF16)

    def write_pair(b, rows):
        out_ref[:, pair_rows(b), :] = rows.astype(BF16)

    inverse_of(product_at, third_ref, last_ref, narrow, scale, write_pair)


def backward_kernel(steps, scale, factor, gate_ref, spectra_ref, first_ref, second_ref, third_ref, last_ref, out_ref, section, gate_spectrum, wide):
    def read_pair(b):
        return gate_ref[:, pair_rows(b), :].astype(F32)

    def store(k, plane):
        gate_spectrum[k] = plane

    spectra_of(read_pair, first_ref, second_ref, section, store)

    def product_at(k):
        both = spectra_ref[k]
        gate = gate_spectrum[k]
        gate = jnp.concatenate([gate, gate], axis=1)
        br, bi, gr, gi = both[:steps], both[steps:], gate[:steps], gate[steps:]
        full = jnp.concatenate([br * gr + bi * gi, br * gi - bi * gr], axis=0)
        return jnp.concatenate([full[:, :LANES], full[:, LANES:] * factor], axis=1).astype(BF16)

    def write_pair(b, rows):
        out_ref[:, pair_rows(b), :] = rows[:, :, :LANES].astype(BF16)
        out_ref[:, pair_rows(b + steps // (2 * SUBLANES)), :] = rows[:, :, LANES:].astype(BF16)

    inverse_of(product_at, third_ref, last_ref, wide, scale, write_pair)


def mixing_kernel(conv_ref, query_ref, grad_ref, key_ref, value_ref, gain_ref, layer_ref, query_grad_ref):
    for j in range(conv_ref.shape[0]):
        cols = pl.ds(j * LANES, LANES)
        product = (key_ref[:, cols].astype(F32) * value_ref[:, cols].astype(F32)).astype(BF16).astype(F32)
        mixing = conv_ref[j].astype(F32) + gain_ref[:, cols] * product
        layer_ref[:, cols] = (query_ref[:, cols].astype(F32) * mixing).astype(BF16)
        query_grad_ref[:, cols] = (grad_ref[:, cols].astype(F32) * mixing).astype(BF16)


def carried_kernel(back_ref, query_ref, grad_ref, key_ref, value_ref, gain_ref, key_grad_ref, value_grad_ref, filter_grad_ref):
    tokens = query_ref.shape[0]
    for j in range(back_ref.shape[0]):
        cols = pl.ds(j * LANES, LANES)
        gate = grad_ref[:, cols].astype(F32) * query_ref[:, cols].astype(F32)
        carried = back_ref[j, :tokens, :].astype(F32) + gain_ref[:, cols] * gate
        key_grad_ref[:, cols] = (carried * value_ref[:, cols].astype(F32)).astype(BF16)
        value_grad_ref[:, cols] = (carried * key_ref[:, cols].astype(F32)).astype(BF16)
        filter_grad_ref[:, cols] = back_ref[j, tokens:, :]


def exchange(blocks):
    return lax.all_to_all(blocks, AXES, split_axis=0, concat_axis=0, tiled=True)


def limit(mib):
    return pltpu.CompilerParams(vmem_limit_bytes=mib * 1024 * 1024)


def channel_body(query_rows, key_rows, value_rows, out_grad, filter_rows, skip_gain):
    devices = lax.axis_size(AXES)
    tokens, channels = query_rows.shape
    length = tokens * devices
    factor = 1.0 / math.sqrt(length)
    scale = 1.0 / (2 * length)
    planes = devices + 1
    first, second, third, last = (jnp.asarray(t) for t in make_tables(devices, tokens))
    group = math.gcd(devices, 8)
    grid = (devices // group,)
    rows_spec = pl.BlockSpec((tokens, group * LANES), lambda i: (0, i))
    vector_spec = pl.BlockSpec((1, group * LANES), lambda i: (0, i))
    single_spec = pl.BlockSpec((group, tokens, LANES), lambda i: (i, 0, 0))
    double_spec = pl.BlockSpec((group, 2 * tokens, LANES), lambda i: (i, 0, 0))
    rows_shape = jax.ShapeDtypeStruct((tokens, channels), BF16)
    single_shape = jax.ShapeDtypeStruct((devices, tokens, LANES), BF16)
    double_shape = jax.ShapeDtypeStruct((devices, 2 * tokens, LANES), BF16)

    packed = pl.pallas_call(
        pack_kernel, grid=grid, in_specs=[rows_spec] * 3, out_specs=double_spec, out_shape=double_shape,
    )(filter_rows, key_rows, value_rows)
    packed = exchange(packed)
    gate, skip_part = pl.pallas_call(
        gate_kernel, grid=grid, in_specs=[rows_spec] * 4, out_specs=[single_spec, vector_spec],
        out_shape=[single_shape, jax.ShapeDtypeStruct((1, channels), F32)],
    )(query_rows, out_grad, key_rows, value_rows)
    skip_parts = lax.all_gather(skip_part, AXES, axis=0, tiled=True)
    gate = exchange(gate)
    convolved, spectra = pl.pallas_call(
        functools.partial(forward_kernel, tokens, scale),
        out_shape=[single_shape, jax.ShapeDtypeStruct((planes, 2 * tokens, 2 * LANES), F32)],
        scratch_shapes=[
            pltpu.VMEM((planes, 2 * tokens, 2 * LANES), F32),
            pltpu.VMEM((planes, 2 * tokens, LANES), F32),
        ],
        compiler_params=limit(48),
    )(packed, first, second, third, last)
    convolved = exchange(convolved)
    back = pl.pallas_call(
        functools.partial(backward_kernel, tokens, scale, factor),
        out_shape=double_shape,
        scratch_shapes=[
            pltpu.VMEM((planes, 2 * tokens, LANES), F32),
            pltpu.VMEM((planes, 2 * tokens, LANES), F32),
            pltpu.VMEM((planes, 2 * tokens, 2 * LANES), F32),
        ],
        compiler_params=limit(48),
    )(gate, spectra, first, second, third, last)
    back = exchange(back)
    gain = skip_gain[None, :]
    layer_out, query_grad = pl.pallas_call(
        mixing_kernel, grid=grid, in_specs=[single_spec] + [rows_spec] * 4 + [vector_spec],
        out_specs=[rows_spec] * 2, out_shape=[rows_shape] * 2,
    )(convolved, query_rows, out_grad, key_rows, value_rows, gain)
    key_grad, value_grad, filter_grad = pl.pallas_call(
        carried_kernel, grid=grid, in_specs=[double_spec] + [rows_spec] * 4 + [vector_spec],
        out_specs=[rows_spec] * 3, out_shape=[rows_shape] * 3,
    )(back, query_rows, out_grad, key_rows, value_rows, gain)
    skip_grad = jnp.sum(skip_parts, axis=0) * factor
    return (layer_out, query_grad, key_grad, value_grad, filter_grad, skip_grad)


def rounded_trig(phase, modulus):
    angle = (phase % modulus).astype(jnp.float32) * (TWO_PI / modulus)
    return (jnp.cos(angle).astype(jnp.bfloat16), jnp.sin(angle).astype(jnp.bfloat16))


def regroup_blocks(blocks):
    return lax.all_to_all(blocks, ("outer", "inner"), split_axis=0, concat_axis=0, tiled=True)


def frequency_body(query_rows, key_rows, value_rows, out_grad, filter_rows, skip_gain):
    devices = lax.axis_size(("outer", "inner"))
    position = lax.axis_index(("outer", "inner"))
    tokens_here = query_rows.shape[0]
    channels = query_rows.shape[1]
    piece_rows = tokens_here // devices
    length = tokens_here * devices
    points = 2 * length
    radix_count = 2 * devices
    factor = 1.0 / math.sqrt(length)
    product = (key_rows.astype(jnp.float32) * value_rows.astype(jnp.float32)).astype(jnp.bfloat16)
    gate_grad = out_grad.astype(jnp.float32) * query_rows.astype(jnp.float32)
    signals = jnp.stack([product, gate_grad.astype(jnp.bfloat16), filter_rows], axis=1)
    columns = regroup_blocks(signals.reshape(devices, piece_rows, 3, channels))
    anchor = jnp.arange(devices, dtype=jnp.int32)
    halves = jnp.arange(2, dtype=jnp.int32)
    local_steps = jnp.arange(piece_rows, dtype=jnp.int32)
    step_index = jnp.arange(tokens_here, dtype=jnp.int32)
    sample = position * piece_rows + local_steps
    section_one = []
    for half in range(2):
        freq_one = half * devices + anchor
        phase = (
            anchor[None, None, :] * freq_one[None, :, None] * tokens_here
            + sample[:, None, None] * freq_one[None, :, None]
        )
        one_cos, one_sin = rounded_trig(phase, points)
        table_one = jnp.stack([one_cos, -one_sin], axis=2).reshape(piece_rows, 2 * devices, devices)
        result = jnp.einsum(
            "skr,rsbc->ksbc", table_one, columns, preferred_element_type=jnp.float32
        )
        section_one.append(result.astype(jnp.bfloat16).reshape(devices, 2, piece_rows, 3, channels))
    section_one = regroup_blocks(jnp.stack(section_one, axis=2))
    full_sample = anchor[:, None] * piece_rows + local_steps[None, :]
    step_cos, step_sin = rounded_trig(
        full_sample[:, :, None] * step_index[None, None, :], tokens_here
    )
    real_col = jnp.stack([step_cos, step_sin])
    imag_col = jnp.stack([-step_sin, step_cos])
    table_two = jnp.stack([real_col, imag_col], axis=3)
    section_three = []
    for half in range(2):
        spectra = jnp.einsum(
            "oisbc,iosjk->jkbc",
            section_one[:, :, half],
            table_two,
            preferred_element_type=jnp.float32,
        )
        spec_real, spec_imag = (spectra[0], spectra[1])
        value_real, gate_real, filter_real = (spec_real[:, 0], spec_real[:, 1], spec_real[:, 2])
        value_imag, gate_imag, filter_imag = (spec_imag[:, 0], spec_imag[:, 1], spec_imag[:, 2])
        forward_real = value_real * filter_real - value_imag * filter_imag
        forward_imag = value_real * filter_imag + value_imag * filter_real
        backward_real = filter_real * gate_real + filter_imag * gate_imag
        backward_imag = filter_real * gate_imag - filter_imag * gate_real
        lag_real = (value_real * gate_real + value_imag * gate_imag) * factor
        lag_imag = (value_real * gate_imag - value_imag * gate_real) * factor
        products = jnp.stack(
            [
                jnp.stack([forward_real, backward_real, lag_real], axis=1),
                jnp.stack([forward_imag, backward_imag, lag_imag], axis=1),
            ]
        ).astype(jnp.bfloat16)
        freq_held = half * devices + position
        phase_three = (
            step_index[None, :] * step_index[:, None] * radix_count
            + step_index[None, :] * freq_held
        )
        three_cos, three_sin = rounded_trig(phase_three, points)
        real_row = jnp.stack([three_cos, -three_sin])
        imag_row = jnp.stack([three_sin, three_cos])
        table_three = jnp.stack([real_row, imag_row], axis=2)
        result = jnp.einsum(
            "ikbc,ikjs->sjbc", products, table_three, preferred_element_type=jnp.float32
        )
        section_three.append(result.astype(jnp.bfloat16))
    section_three = jnp.stack(section_three, axis=2).reshape(devices, piece_rows, 2, 2, 3, channels)
    rows_back = regroup_blocks(section_three)
    freq_last = halves[:, None] * devices + anchor[None, :]
    last_cos, last_sin = rounded_trig(anchor[None, None, :] * freq_last[:, :, None], radix_count)
    table_four = jnp.stack([last_cos, -last_sin])
    restored = (
        jnp.einsum("opjhbc,jhor->rpbc", rows_back, table_four, preferred_element_type=jnp.float32)
        / points
    )
    home_rows = regroup_blocks(restored.astype(jnp.bfloat16)).reshape(tokens_here, 3, channels)
    convolved = home_rows[:, 0].astype(jnp.float32)
    correlated = home_rows[:, 1].astype(jnp.float32)
    filter_grad = home_rows[:, 2]
    product_full = product.astype(jnp.float32)
    mixing = convolved + skip_gain[None, :] * product_full
    layer_out = (query_rows.astype(jnp.float32) * mixing).astype(jnp.bfloat16)
    query_grad = (out_grad.astype(jnp.float32) * mixing).astype(jnp.bfloat16)
    carried = correlated + skip_gain[None, :] * gate_grad
    key_grad = (carried * value_rows.astype(jnp.float32)).astype(jnp.bfloat16)
    value_grad = (carried * key_rows.astype(jnp.float32)).astype(jnp.bfloat16)
    skip_part = jnp.sum(gate_grad * product_full, axis=0)
    skip_sum = lax.psum(skip_part, ("outer", "inner"))
    return (layer_out, query_grad, key_grad, value_grad, filter_grad, skip_sum * factor)


def body(*arrays):
    lanes_full = arrays[0].shape[1] == lax.axis_size(AXES) * LANES
    return (channel_body if lanes_full else frequency_body)(*arrays)


def solution(mesh):
    return jax.shard_map(
        body,
        mesh=mesh,
        in_specs=(
            P(("outer", "inner"), None),
            P(("outer", "inner"), None),
            P(("outer", "inner"), None),
            P(("outer", "inner"), None),
            P(("outer", "inner"), None),
            P(),
        ),
        out_specs=(
            P(("outer", "inner"), None),
            P(("outer", "inner"), None),
            P(("outer", "inner"), None),
            P(("outer", "inner"), None),
            P(("outer", "inner"), None),
            P(),
        ),
        check_vma=False,
    )
```

```python
import functools
import math

import jax
import jax.numpy as jnp
import ml_dtypes
import numpy as np
from jax import lax
from jax.experimental import pallas as pl
from jax.experimental.pallas import tpu as pltpu
from jax.sharding import PartitionSpec as P

TWO_PI = 2.0 * math.pi
AXES = ("outer", "inner")
LANES = 128
SUBLANES = 8
BF16 = jnp.bfloat16
F32 = jnp.float32


def table_trig(phase, modulus):
    angle = (phase % modulus).astype(np.float32) * np.float32(TWO_PI / modulus)
    return tuple(
        part.astype(ml_dtypes.bfloat16).astype(np.float32) for part in (np.cos(angle), np.sin(angle))
    )


def make_tables(rows, steps):
    planes = rows + 1
    points = 2 * rows * steps
    row = np.arange(rows)
    plane = np.arange(planes)
    step = np.arange(steps)
    eye = np.eye(SUBLANES, dtype=np.float32)
    phase = row[None, None, :] * plane[None, :, None] * steps + step[:, None, None] * plane[None, :, None]
    cos, sin = table_trig(phase, points)
    first = np.stack([cos, -sin], axis=1).reshape(steps // SUBLANES, SUBLANES, 2, planes, rows)
    first = np.einsum("bipkr,ij->bpkirj", first, eye)
    first = first.reshape(steps // SUBLANES, 2 * planes * SUBLANES, rows * SUBLANES)
    cos, sin = table_trig(step[:, None] * step[None, :], steps)
    second = np.block([[cos, sin], [-sin, cos]])
    phase = step[None, :, None] * step[None, None, :] * (2 * rows) + step[None, :, None] * plane[:, None, None]
    cos, sin = table_trig(phase, points)
    third = np.concatenate(
        [np.concatenate([cos, -sin], axis=2), np.concatenate([sin, cos], axis=2)], axis=1
    )
    cos, sin = table_trig(row[:, None] * plane[None, :], 2 * rows)
    weight = np.where((plane == 0) | (plane == rows), 1.0, 2.0).astype(np.float32)
    last = np.stack([cos * weight, -sin * weight], axis=1)
    last = np.einsum("rpk,ij->ripkj", last, eye).reshape(rows * SUBLANES, 2 * planes * SUBLANES)
    return tuple(table.astype(ml_dtypes.bfloat16) for table in (first, second, third, last))


def dot(a, b):
    return jnp.dot(a, b, preferred_element_type=F32)


def pack_kernel(filter_ref, key_ref, value_ref, out_ref):
    blocks = out_ref.shape[0]
    tokens = filter_ref.shape[0]
    for j in range(blocks):
        cols = pl.ds(j * LANES, LANES)
        out_ref[j, :tokens, :] = filter_ref[:, cols]
        product = key_ref[:, cols].astype(F32) * value_ref[:, cols].astype(F32)
        out_ref[j, tokens:, :] = product.astype(BF16)


def gate_kernel(query_ref, grad_ref, key_ref, value_ref, out_ref, skip_ref):
    blocks = out_ref.shape[0]
    for j in range(blocks):
        cols = pl.ds(j * LANES, LANES)
        gate = grad_ref[:, cols].astype(F32) * query_ref[:, cols].astype(F32)
        product = (key_ref[:, cols].astype(F32) * value_ref[:, cols].astype(F32)).astype(BF16).astype(F32)
        out_ref[j] = gate.astype(BF16)
        skip_ref[:, cols] = jnp.sum(gate * product, axis=0, keepdims=True)


def spectra_of(read_pair, first_ref, second_ref, section, store):
    planes = section.shape[0]
    steps = section.shape[1] // 2
    width = section.shape[2]

    def one(b, _):
        pair = read_pair(b)
        for half in range(2):
            block = pair[:, half * SUBLANES : (half + 1) * SUBLANES, :]
            flat = block.reshape(-1, width).astype(BF16)
            result = dot(first_ref[2 * b + half], flat).reshape(2, planes, SUBLANES, width)
            at = pl.multiple_of((2 * b + half) * SUBLANES, SUBLANES)
            section[:, pl.ds(at, SUBLANES), :] = result[0]
            section[:, pl.ds(steps + at, SUBLANES), :] = result[1]
        return 0

    lax.fori_loop(0, steps // (2 * SUBLANES), one, 0)

    def two(k, _):
        store(k, dot(second_ref[...], section[k].astype(BF16)))
        return 0

    lax.fori_loop(0, planes, two, 0)


def inverse_of(product_at, third_ref, last_ref, section, scale, write_pair):
    planes = section.shape[0]
    steps = section.shape[1] // 2
    width = section.shape[2]

    def three(k, _):
        section[k] = dot(third_ref[k], product_at(k))
        return 0

    lax.fori_loop(0, planes, three, 0)

    def four(b, _):
        halves = []
        for half in range(2):
            at = pl.multiple_of((2 * b + half) * SUBLANES, SUBLANES)
            real = section[:, pl.ds(at, SUBLANES), :].reshape(-1, width)
            imag = section[:, pl.ds(steps + at, SUBLANES), :].reshape(-1, width)
            flat = jnp.concatenate([real, imag], axis=0).astype(BF16)
            halves.append((dot(last_ref[...], flat) * scale).reshape(-1, SUBLANES, width))
        write_pair(b, jnp.concatenate(halves, axis=1))
        return 0

    lax.fori_loop(0, steps // (2 * SUBLANES), four, 0)


def pair_rows(b):
    return pl.ds(pl.multiple_of(b * 2 * SUBLANES, 2 * SUBLANES), 2 * SUBLANES)


def forward_kernel(steps, scale, packed_ref, first_ref, second_ref, third_ref, last_ref, out_ref, spectra_ref, section, narrow):
    def read_pair(b):
        return jnp.concatenate(
            [
                packed_ref[:, pair_rows(b), :].astype(F32),
                packed_ref[:, pair_rows(b + steps // (2 * SUBLANES)), :].astype(F32),
            ],
            axis=2,
        )

    def store(k, plane):
        spectra_ref[k] = plane

    spectra_of(read_pair, first_ref, second_ref, section, store)

    def product_at(k):
        filt = spectra_ref[k, :, :LANES]
        value = spectra_ref[k, :, LANES:]
        fr, fi, vr, vi = filt[:steps], filt[steps:], value[:steps], value[steps:]
        return jnp.concatenate([vr * fr - vi * fi, vr * fi + vi * fr], axis=0).astype(BF16)

    def write_pair(b, rows):
        out_ref[:, pair_rows(b), :] = rows.astype(BF16)

    inverse_of(product_at, third_ref, last_ref, narrow, scale, write_pair)


def backward_kernel(steps, scale, factor, gate_ref, spectra_ref, first_ref, second_ref, third_ref, last_ref, out_ref, section, gate_spectrum, wide):
    def read_pair(b):
        return gate_ref[:, pair_rows(b), :].astype(F32)

    def store(k, plane):
        gate_spectrum[k] = plane

    spectra_of(read_pair, first_ref, second_ref, section, store)

    def product_at(k):
        both = spectra_ref[k]
        gate = gate_spectrum[k]
        gate = jnp.concatenate([gate, gate], axis=1)
        br, bi, gr, gi = both[:steps], both[steps:], gate[:steps], gate[steps:]
        full = jnp.concatenate([br * gr + bi * gi, br * gi - bi * gr], axis=0)
        return jnp.concatenate([full[:, :LANES], full[:, LANES:] * factor], axis=1).astype(BF16)

    def write_pair(b, rows):
        out_ref[:, pair_rows(b), :] = rows[:, :, :LANES].astype(BF16)
        out_ref[:, pair_rows(b + steps // (2 * SUBLANES)), :] = rows[:, :, LANES:].astype(BF16)

    inverse_of(product_at, third_ref, last_ref, wide, scale, write_pair)


def mixing_kernel(conv_ref, query_ref, grad_ref, key_ref, value_ref, gain_ref, layer_ref, query_grad_ref):
    for j in range(conv_ref.shape[0]):
        cols = pl.ds(j * LANES, LANES)
        product = (key_ref[:, cols].astype(F32) * value_ref[:, cols].astype(F32)).astype(BF16).astype(F32)
        mixing = conv_ref[j].astype(F32) + gain_ref[:, cols] * product
        layer_ref[:, cols] = (query_ref[:, cols].astype(F32) * mixing).astype(BF16)
        query_grad_ref[:, cols] = (grad_ref[:, cols].astype(F32) * mixing).astype(BF16)


def carried_kernel(back_ref, query_ref, grad_ref, key_ref, value_ref, gain_ref, key_grad_ref, value_grad_ref, filter_grad_ref):
    tokens = query_ref.shape[0]
    for j in range(back_ref.shape[0]):
        cols = pl.ds(j * LANES, LANES)
        gate = grad_ref[:, cols].astype(F32) * query_ref[:, cols].astype(F32)
        carried = back_ref[j, :tokens, :].astype(F32) + gain_ref[:, cols] * gate
        key_grad_ref[:, cols] = (carried * value_ref[:, cols].astype(F32)).astype(BF16)
        value_grad_ref[:, cols] = (carried * key_ref[:, cols].astype(F32)).astype(BF16)
        filter_grad_ref[:, cols] = back_ref[j, tokens:, :]


def exchange(blocks):
    return lax.all_to_all(blocks, AXES, split_axis=0, concat_axis=0, tiled=True)


def total_of(part):
    devices = lax.axis_size(AXES)
    step = 1
    while step < devices:
        part = part + lax.ppermute(part, AXES, [(d, d ^ step) for d in range(devices)])
        step *= 2
    return part


def limit(mib):
    return pltpu.CompilerParams(vmem_limit_bytes=mib * 1024 * 1024)


def channel_body(query_rows, key_rows, value_rows, out_grad, filter_rows, skip_gain):
    devices = lax.axis_size(AXES)
    tokens, channels = query_rows.shape
    length = tokens * devices
    factor = 1.0 / math.sqrt(length)
    scale = 1.0 / (2 * length)
    planes = devices + 1
    first, second, third, last = (jnp.asarray(t) for t in make_tables(devices, tokens))
    group = math.gcd(devices, 8)
    grid = (devices // group,)
    rows_spec = pl.BlockSpec((tokens, group * LANES), lambda i: (0, i))
    vector_spec = pl.BlockSpec((1, group * LANES), lambda i: (0, i))
    single_spec = pl.BlockSpec((group, tokens, LANES), lambda i: (i, 0, 0))
    double_spec = pl.BlockSpec((group, 2 * tokens, LANES), lambda i: (i, 0, 0))
    rows_shape = jax.ShapeDtypeStruct((tokens, channels), BF16)
    single_shape = jax.ShapeDtypeStruct((devices, tokens, LANES), BF16)
    double_shape = jax.ShapeDtypeStruct((devices, 2 * tokens, LANES), BF16)

    packed = pl.pallas_call(
        pack_kernel, grid=grid, in_specs=[rows_spec] * 3, out_specs=double_spec, out_shape=double_shape,
    )(filter_rows, key_rows, value_rows)
    packed = exchange(packed)
    gate, skip_part = pl.pallas_call(
        gate_kernel, grid=grid, in_specs=[rows_spec] * 4, out_specs=[single_spec, vector_spec],
        out_shape=[single_shape, jax.ShapeDtypeStruct((1, channels), F32)],
    )(query_rows, out_grad, key_rows, value_rows)
    skip_total = total_of(skip_part)
    gate = exchange(gate)
    convolved, spectra = pl.pallas_call(
        functools.partial(forward_kernel, tokens, scale),
        out_shape=[single_shape, jax.ShapeDtypeStruct((planes, 2 * tokens, 2 * LANES), F32)],
        scratch_shapes=[
            pltpu.VMEM((planes, 2 * tokens, 2 * LANES), F32),
            pltpu.VMEM((planes, 2 * tokens, LANES), F32),
        ],
        compiler_params=limit(48),
    )(packed, first, second, third, last)
    convolved = exchange(convolved)
    back = pl.pallas_call(
        functools.partial(backward_kernel, tokens, scale, factor),
        out_shape=double_shape,
        scratch_shapes=[
            pltpu.VMEM((planes, 2 * tokens, LANES), F32),
            pltpu.VMEM((planes, 2 * tokens, LANES), F32),
            pltpu.VMEM((planes, 2 * tokens, 2 * LANES), F32),
        ],
        compiler_params=limit(48),
    )(gate, spectra, first, second, third, last)
    back = exchange(back)
    gain = skip_gain[None, :]
    layer_out, query_grad = pl.pallas_call(
        mixing_kernel, grid=grid, in_specs=[single_spec] + [rows_spec] * 4 + [vector_spec],
        out_specs=[rows_spec] * 2, out_shape=[rows_shape] * 2,
    )(convolved, query_rows, out_grad, key_rows, value_rows, gain)
    key_grad, value_grad, filter_grad = pl.pallas_call(
        carried_kernel, grid=grid, in_specs=[double_spec] + [rows_spec] * 4 + [vector_spec],
        out_specs=[rows_spec] * 3, out_shape=[rows_shape] * 3,
    )(back, query_rows, out_grad, key_rows, value_rows, gain)
    skip_grad = skip_total[0] * factor
    return (layer_out, query_grad, key_grad, value_grad, filter_grad, skip_grad)


def rounded_trig(phase, modulus):
    angle = (phase % modulus).astype(jnp.float32) * (TWO_PI / modulus)
    return (jnp.cos(angle).astype(jnp.bfloat16), jnp.sin(angle).astype(jnp.bfloat16))


def regroup_blocks(blocks):
    return lax.all_to_all(blocks, ("outer", "inner"), split_axis=0, concat_axis=0, tiled=True)


def frequency_body(query_rows, key_rows, value_rows, out_grad, filter_rows, skip_gain):
    devices = lax.axis_size(("outer", "inner"))
    position = lax.axis_index(("outer", "inner"))
    tokens_here = query_rows.shape[0]
    channels = query_rows.shape[1]
    piece_rows = tokens_here // devices
    length = tokens_here * devices
    points = 2 * length
    radix_count = 2 * devices
    factor = 1.0 / math.sqrt(length)
    product = (key_rows.astype(jnp.float32) * value_rows.astype(jnp.float32)).astype(jnp.bfloat16)
    gate_grad = out_grad.astype(jnp.float32) * query_rows.astype(jnp.float32)
    signals = jnp.stack([product, gate_grad.astype(jnp.bfloat16), filter_rows], axis=1)
    columns = regroup_blocks(signals.reshape(devices, piece_rows, 3, channels))
    anchor = jnp.arange(devices, dtype=jnp.int32)
    halves = jnp.arange(2, dtype=jnp.int32)
    local_steps = jnp.arange(piece_rows, dtype=jnp.int32)
    step_index = jnp.arange(tokens_here, dtype=jnp.int32)
    sample = position * piece_rows + local_steps
    section_one = []
    for half in range(2):
        freq_one = half * devices + anchor
        phase = (
            anchor[None, None, :] * freq_one[None, :, None] * tokens_here
            + sample[:, None, None] * freq_one[None, :, None]
        )
        one_cos, one_sin = rounded_trig(phase, points)
        table_one = jnp.stack([one_cos, -one_sin], axis=2).reshape(piece_rows, 2 * devices, devices)
        result = jnp.einsum(
            "skr,rsbc->ksbc", table_one, columns, preferred_element_type=jnp.float32
        )
        section_one.append(result.astype(jnp.bfloat16).reshape(devices, 2, piece_rows, 3, channels))
    section_one = regroup_blocks(jnp.stack(section_one, axis=2))
    full_sample = anchor[:, None] * piece_rows + local_steps[None, :]
    step_cos, step_sin = rounded_trig(
        full_sample[:, :, None] * step_index[None, None, :], tokens_here
    )
    real_col = jnp.stack([step_cos, step_sin])
    imag_col = jnp.stack([-step_sin, step_cos])
    table_two = jnp.stack([real_col, imag_col], axis=3)
    section_three = []
    for half in range(2):
        spectra = jnp.einsum(
            "oisbc,iosjk->jkbc",
            section_one[:, :, half],
            table_two,
            preferred_element_type=jnp.float32,
        )
        spec_real, spec_imag = (spectra[0], spectra[1])
        value_real, gate_real, filter_real = (spec_real[:, 0], spec_real[:, 1], spec_real[:, 2])
        value_imag, gate_imag, filter_imag = (spec_imag[:, 0], spec_imag[:, 1], spec_imag[:, 2])
        forward_real = value_real * filter_real - value_imag * filter_imag
        forward_imag = value_real * filter_imag + value_imag * filter_real
        backward_real = filter_real * gate_real + filter_imag * gate_imag
        backward_imag = filter_real * gate_imag - filter_imag * gate_real
        lag_real = (value_real * gate_real + value_imag * gate_imag) * factor
        lag_imag = (value_real * gate_imag - value_imag * gate_real) * factor
        products = jnp.stack(
            [
                jnp.stack([forward_real, backward_real, lag_real], axis=1),
                jnp.stack([forward_imag, backward_imag, lag_imag], axis=1),
            ]
        ).astype(jnp.bfloat16)
        freq_held = half * devices + position
        phase_three = (
            step_index[None, :] * step_index[:, None] * radix_count
            + step_index[None, :] * freq_held
        )
        three_cos, three_sin = rounded_trig(phase_three, points)
        real_row = jnp.stack([three_cos, -three_sin])
        imag_row = jnp.stack([three_sin, three_cos])
        table_three = jnp.stack([real_row, imag_row], axis=2)
        result = jnp.einsum(
            "ikbc,ikjs->sjbc", products, table_three, preferred_element_type=jnp.float32
        )
        section_three.append(result.astype(jnp.bfloat16))
    section_three = jnp.stack(section_three, axis=2).reshape(devices, piece_rows, 2, 2, 3, channels)
    rows_back = regroup_blocks(section_three)
    freq_last = halves[:, None] * devices + anchor[None, :]
    last_cos, last_sin = rounded_trig(anchor[None, None, :] * freq_last[:, :, None], radix_count)
    table_four = jnp.stack([last_cos, -last_sin])
    restored = (
        jnp.einsum("opjhbc,jhor->rpbc", rows_back, table_four, preferred_element_type=jnp.float32)
        / points
    )
    home_rows = regroup_blocks(restored.astype(jnp.bfloat16)).reshape(tokens_here, 3, channels)
    convolved = home_rows[:, 0].astype(jnp.float32)
    correlated = home_rows[:, 1].astype(jnp.float32)
    filter_grad = home_rows[:, 2]
    product_full = product.astype(jnp.float32)
    mixing = convolved + skip_gain[None, :] * product_full
    layer_out = (query_rows.astype(jnp.float32) * mixing).astype(jnp.bfloat16)
    query_grad = (out_grad.astype(jnp.float32) * mixing).astype(jnp.bfloat16)
    carried = correlated + skip_gain[None, :] * gate_grad
    key_grad = (carried * value_rows.astype(jnp.float32)).astype(jnp.bfloat16)
    value_grad = (carried * key_rows.astype(jnp.float32)).astype(jnp.bfloat16)
    skip_part = jnp.sum(gate_grad * product_full, axis=0)
    skip_sum = lax.psum(skip_part, ("outer", "inner"))
    return (layer_out, query_grad, key_grad, value_grad, filter_grad, skip_sum * factor)


def body(*arrays):
    lanes_full = arrays[0].shape[1] == lax.axis_size(AXES) * LANES
    return (channel_body if lanes_full else frequency_body)(*arrays)


def solution(mesh):
    return jax.shard_map(
        body,
        mesh=mesh,
        in_specs=(
            P(("outer", "inner"), None),
            P(("outer", "inner"), None),
            P(("outer", "inner"), None),
            P(("outer", "inner"), None),
            P(("outer", "inner"), None),
            P(),
        ),
        out_specs=(
            P(("outer", "inner"), None),
            P(("outer", "inner"), None),
            P(("outer", "inner"), None),
            P(("outer", "inner"), None),
            P(("outer", "inner"), None),
            P(),
        ),
        check_vma=False,
    )
```

```python
import functools
import math

import jax
import jax.numpy as jnp
import ml_dtypes
import numpy as np
from jax import lax
from jax.experimental import pallas as pl
from jax.experimental.pallas import tpu as pltpu
from jax.sharding import PartitionSpec as P

TWO_PI = 2.0 * math.pi
AXES = ("outer", "inner")
LANES = 128
SUBLANES = 8
SPARE = 2 * SUBLANES
BF16 = jnp.bfloat16
F32 = jnp.float32


def table_trig(phase, modulus):
    angle = (phase % modulus).astype(np.float32) * np.float32(TWO_PI / modulus)
    return tuple(
        part.astype(ml_dtypes.bfloat16).astype(np.float32) for part in (np.cos(angle), np.sin(angle))
    )


def make_tables(rows, steps):
    planes = rows + 1
    points = 2 * rows * steps
    row = np.arange(rows)
    plane = np.arange(planes)
    step = np.arange(steps)
    eye = np.eye(SUBLANES, dtype=np.float32)
    phase = row[None, None, :] * plane[None, :, None] * steps + step[:, None, None] * plane[None, :, None]
    cos, sin = table_trig(phase, points)
    first = np.stack([cos, -sin], axis=1).reshape(steps // SUBLANES, SUBLANES, 2, planes, rows)
    first = np.einsum("bipkr,ij->bpkirj", first, eye)
    first = first.reshape(steps // SUBLANES, 2 * planes * SUBLANES, rows * SUBLANES)
    cos, sin = table_trig(step[:, None] * step[None, :], steps)
    second = np.block([[cos, sin], [-sin, cos]])
    phase = step[None, :, None] * step[None, None, :] * (2 * rows) + step[None, :, None] * plane[:, None, None]
    cos, sin = table_trig(phase, points)
    third = np.concatenate(
        [np.concatenate([cos, -sin], axis=2), np.concatenate([sin, cos], axis=2)], axis=1
    )
    cos, sin = table_trig(row[:, None] * plane[None, :], 2 * rows)
    weight = np.where((plane == 0) | (plane == rows), 1.0, 2.0).astype(np.float32)
    last = np.stack([cos * weight, -sin * weight], axis=1)
    last = np.einsum("rpk,ij->ripkj", last, eye).reshape(rows * SUBLANES, 2 * planes * SUBLANES)
    return tuple(table.astype(ml_dtypes.bfloat16) for table in (first, second, third, last))


def dot(a, b):
    return jnp.dot(a, b, preferred_element_type=F32)


def product_of(key, value):
    return (key.astype(F32) * value.astype(F32)).astype(BF16)


def row_group(b, size=2 * SUBLANES):
    return pl.ds(pl.multiple_of(b * size, size), size)


def pack_kernel(filter_ref, key_ref, value_ref, out_ref):
    tokens = filter_ref.shape[0]
    for d in range(out_ref.shape[0]):
        cols = pl.ds(d * LANES, LANES)
        out_ref[d, :tokens, :] = filter_ref[:, cols]
        out_ref[d, tokens:, :] = product_of(key_ref[:, cols], value_ref[:, cols])


def gate_kernel(query_ref, grad_ref, out_ref):
    for d in range(out_ref.shape[0]):
        cols = pl.ds(d * LANES, LANES)
        out_ref[d] = (grad_ref[:, cols].astype(F32) * query_ref[:, cols].astype(F32)).astype(BF16)


def looped(count, chunk, one):
    def several(i, _):
        for j in range(chunk):
            one(i * chunk + j)
        return 0

    lax.fori_loop(0, count // chunk, several, 0)
    for i in range(count - count % chunk, count):
        one(i)


def spectrum_of(read, first_ref, second_ref, section, store):
    planes, steps, width = section.shape[0], section.shape[1] // 2, section.shape[2]

    def one(b):
        pair = read(b)
        for half in range(2):
            block = pair[:, half * SUBLANES : (half + 1) * SUBLANES, :]
            result = dot(first_ref[2 * b + half], block.reshape(-1, width).astype(BF16))
            result = result.reshape(2, planes, SUBLANES, width)
            section[:, row_group(2 * b + half, SUBLANES), :] = result[0]
            section[:, row_group(2 * b + half + steps // SUBLANES, SUBLANES), :] = result[1]

    looped(steps // (2 * SUBLANES), 2, one)

    def two(k):
        store(k, dot(second_ref[...], section[k].astype(BF16)))

    looped(planes, 8, two)


def inverse_of(product_at, third_ref, last_ref, section, scale, write):
    planes, steps, width = section.shape[0], section.shape[1] // 2, section.shape[2]

    def three(k):
        section[k] = dot(third_ref[k], product_at(k))

    looped(planes, 8, three)

    def four(b):
        halves = []
        for half in range(2):
            real = section[:, row_group(2 * b + half, SUBLANES), :].reshape(-1, width)
            imag = section[:, row_group(2 * b + half + steps // SUBLANES, SUBLANES), :].reshape(-1, width)
            flat = jnp.concatenate([real, imag], axis=0).astype(BF16)
            halves.append((dot(last_ref[...], flat) * scale).reshape(-1, SUBLANES, width))
        write(b, jnp.concatenate(halves, axis=1).astype(BF16))

    looped(steps // (2 * SUBLANES), 2, four)


def parts_of(plane):
    steps = plane.shape[0] // 2
    return plane[:steps], plane[steps:]


def conj_product(a, b):
    (ar, ai), (br, bi) = parts_of(a), parts_of(b)
    return jnp.concatenate([ar * br + ai * bi, ar * bi - ai * br], axis=0)


def forward_kernel(scale, packed_ref, first_ref, second_ref, third_ref, last_ref, out_ref, spectra_ref, wide, narrow):
    pairs = packed_ref.shape[1] // (4 * SUBLANES)

    def read(b):
        filt, value = packed_ref[:, row_group(b), :], packed_ref[:, row_group(b + pairs), :]
        return jnp.concatenate([filt.astype(F32), value.astype(F32)], axis=2)

    def store(k, plane):
        spectra_ref[k] = plane

    spectrum_of(read, first_ref, second_ref, wide, store)

    def product_at(k):
        (fr, fi), (vr, vi) = parts_of(spectra_ref[k, :, :LANES]), parts_of(spectra_ref[k, :, LANES:])
        return jnp.concatenate([vr * fr - vi * fi, vr * fi + vi * fr], axis=0).astype(BF16)

    def write(b, rows):
        out_ref[:, row_group(b), :] = rows

    inverse_of(product_at, third_ref, last_ref, narrow, scale, write)


def split_rows(total):
    rows = []
    for _ in range(3):
        rows.append(total.astype(BF16).astype(F32))
        total = total - rows[-1]
    rows.append(jnp.zeros((SPARE - len(rows), total.shape[1]), F32))
    return jnp.concatenate(rows, axis=0).astype(BF16)


def backward_kernel(scale, factor, gate_ref, packed_ref, spectra_ref, first_ref, second_ref, third_ref, last_ref, out_ref, section, gate_spectrum, wide):
    steps = gate_ref.shape[1]
    pairs = steps // (2 * SUBLANES)

    def gate_times_product(d, total):
        return total + gate_ref[d].astype(F32) * packed_ref[d, steps:, :].astype(F32)

    total = lax.fori_loop(0, gate_ref.shape[0], gate_times_product, jnp.zeros((steps, LANES), F32))
    spare = split_rows(jnp.sum(total, axis=0, keepdims=True) * factor)
    for d in range(out_ref.shape[0]):
        out_ref[d, 2 * steps :, :] = spare

    def read(b):
        return gate_ref[:, row_group(b), :].astype(F32)

    def store(k, plane):
        gate_spectrum[k] = plane

    spectrum_of(read, first_ref, second_ref, section, store)

    def product_at(k):
        gate = gate_spectrum[k]
        back = conj_product(spectra_ref[k, :, :LANES], gate)
        lag = conj_product(spectra_ref[k, :, LANES:], gate) * factor
        return jnp.concatenate([back, lag], axis=1).astype(BF16)

    def write(b, rows):
        out_ref[:, row_group(b), :] = rows[:, :, :LANES]
        out_ref[:, row_group(b + pairs), :] = rows[:, :, LANES:]

    inverse_of(product_at, third_ref, last_ref, wide, scale, write)


def mixing_kernel(conv_ref, query_ref, grad_ref, key_ref, value_ref, gain_ref, layer_ref, query_grad_ref):
    for d in range(conv_ref.shape[0]):
        cols = pl.ds(d * LANES, LANES)
        product = product_of(key_ref[:, cols], value_ref[:, cols]).astype(F32)
        mixing = conv_ref[d].astype(F32) + gain_ref[:, cols] * product
        layer_ref[:, cols] = (query_ref[:, cols].astype(F32) * mixing).astype(BF16)
        query_grad_ref[:, cols] = (grad_ref[:, cols].astype(F32) * mixing).astype(BF16)


def carried_kernel(back_ref, query_ref, grad_ref, key_ref, value_ref, gain_ref, key_grad_ref, value_grad_ref, filter_grad_ref, skip_ref):
    tokens = query_ref.shape[0]
    for d in range(back_ref.shape[0]):
        cols = pl.ds(d * LANES, LANES)
        gate = grad_ref[:, cols].astype(F32) * query_ref[:, cols].astype(F32)
        carried = back_ref[d, :tokens, :].astype(F32) + gain_ref[:, cols] * gate
        key_grad_ref[:, cols] = (carried * value_ref[:, cols].astype(F32)).astype(BF16)
        value_grad_ref[:, cols] = (carried * key_ref[:, cols].astype(F32)).astype(BF16)
        filter_grad_ref[:, cols] = back_ref[d, tokens : 2 * tokens, :]
        spare = back_ref[d, 2 * tokens :, :].astype(F32)
        skip_ref[:, cols] = jnp.sum(spare, axis=0, keepdims=True)


def exchange(blocks):
    return lax.all_to_all(blocks, AXES, split_axis=0, concat_axis=0, tiled=True)


def limit(mib):
    return pltpu.CompilerParams(vmem_limit_bytes=mib * 1024 * 1024)


def kernel(body, *arrays, after=(), in_specs=None, **options):
    count, waits = len(arrays), len(after)

    def waiting(*refs):
        body(*refs[:count], *refs[count + waits :])

    specs = list(in_specs or [pl.BlockSpec()] * count) + [pl.BlockSpec(memory_space=pl.ANY)] * waits
    return pl.pallas_call(waiting, in_specs=specs, **options)(*arrays, *after)


def channel_body(query_rows, key_rows, value_rows, out_grad, filter_rows, skip_gain):
    devices = lax.axis_size(AXES)
    tokens, channels = query_rows.shape
    length = tokens * devices
    factor = 1.0 / math.sqrt(length)
    scale = 1.0 / (2 * length)
    planes = devices + 1
    tables = [jnp.asarray(table) for table in make_tables(devices, tokens)]
    blocks = math.gcd(devices, 8)
    grid = (devices // blocks,)
    back_rows = 2 * tokens + SPARE
    rows_spec = pl.BlockSpec((tokens, blocks * LANES), lambda i: (0, i))
    vector_spec = pl.BlockSpec((1, blocks * LANES), lambda i: (0, i))
    single_spec = pl.BlockSpec((blocks, tokens, LANES), lambda i: (i, 0, 0))
    double_spec = pl.BlockSpec((blocks, 2 * tokens, LANES), lambda i: (i, 0, 0))
    back_spec = pl.BlockSpec((blocks, back_rows, LANES), lambda i: (i, 0, 0))
    rows_shape = jax.ShapeDtypeStruct((tokens, channels), BF16)
    single_shape = jax.ShapeDtypeStruct((devices, tokens, LANES), BF16)
    double_shape = jax.ShapeDtypeStruct((devices, 2 * tokens, LANES), BF16)
    back_shape = jax.ShapeDtypeStruct((devices, back_rows, LANES), BF16)
    narrow = pltpu.VMEM((planes, 2 * tokens, LANES), F32)
    wide = pltpu.VMEM((planes, 2 * tokens, 2 * LANES), F32)

    packed = kernel(
        pack_kernel, filter_rows, key_rows, value_rows, grid=grid,
        in_specs=[rows_spec] * 3, out_specs=double_spec, out_shape=double_shape,
    )
    gate = kernel(
        gate_kernel, query_rows, out_grad, after=[packed], grid=grid,
        in_specs=[rows_spec] * 2, out_specs=single_spec, out_shape=single_shape,
    )
    packed = exchange(packed)
    gate = exchange(gate)
    convolved, spectra = kernel(
        functools.partial(forward_kernel, scale), packed, *tables,
        out_shape=[single_shape, jax.ShapeDtypeStruct((planes, 2 * tokens, 2 * LANES), F32)],
        scratch_shapes=[wide, narrow], compiler_params=limit(48),
    )
    convolved = exchange(convolved)
    back = kernel(
        functools.partial(backward_kernel, scale, factor), gate, packed, spectra, *tables,
        out_shape=back_shape, scratch_shapes=[narrow, narrow, wide], compiler_params=limit(52),
    )
    back = exchange(back)
    branches = (query_rows, out_grad, key_rows, value_rows, skip_gain[None, :])
    branch_specs = [rows_spec] * 4 + [vector_spec]
    layer_out, query_grad = kernel(
        mixing_kernel, convolved, *branches, grid=grid, in_specs=[single_spec] + branch_specs,
        out_specs=[rows_spec] * 2, out_shape=[rows_shape] * 2,
    )
    key_grad, value_grad, filter_grad, skip_grad = kernel(
        carried_kernel, back, *branches, after=[layer_out], grid=grid, in_specs=[back_spec] + branch_specs,
        out_specs=[rows_spec] * 3 + [vector_spec],
        out_shape=[rows_shape] * 3 + [jax.ShapeDtypeStruct((1, channels), F32)],
    )
    return (layer_out, query_grad, key_grad, value_grad, filter_grad, skip_grad[0])


def rounded_trig(phase, modulus):
    angle = (phase % modulus).astype(jnp.float32) * (TWO_PI / modulus)
    return (jnp.cos(angle).astype(jnp.bfloat16), jnp.sin(angle).astype(jnp.bfloat16))


def regroup_blocks(blocks):
    return lax.all_to_all(blocks, ("outer", "inner"), split_axis=0, concat_axis=0, tiled=True)


def frequency_body(query_rows, key_rows, value_rows, out_grad, filter_rows, skip_gain):
    devices = lax.axis_size(("outer", "inner"))
    position = lax.axis_index(("outer", "inner"))
    tokens_here = query_rows.shape[0]
    channels = query_rows.shape[1]
    piece_rows = tokens_here // devices
    length = tokens_here * devices
    points = 2 * length
    radix_count = 2 * devices
    factor = 1.0 / math.sqrt(length)
    product = (key_rows.astype(jnp.float32) * value_rows.astype(jnp.float32)).astype(jnp.bfloat16)
    gate_grad = out_grad.astype(jnp.float32) * query_rows.astype(jnp.float32)
    signals = jnp.stack([product, gate_grad.astype(jnp.bfloat16), filter_rows], axis=1)
    columns = regroup_blocks(signals.reshape(devices, piece_rows, 3, channels))
    anchor = jnp.arange(devices, dtype=jnp.int32)
    halves = jnp.arange(2, dtype=jnp.int32)
    local_steps = jnp.arange(piece_rows, dtype=jnp.int32)
    step_index = jnp.arange(tokens_here, dtype=jnp.int32)
    sample = position * piece_rows + local_steps
    section_one = []
    for half in range(2):
        freq_one = half * devices + anchor
        phase = (
            anchor[None, None, :] * freq_one[None, :, None] * tokens_here
            + sample[:, None, None] * freq_one[None, :, None]
        )
        one_cos, one_sin = rounded_trig(phase, points)
        table_one = jnp.stack([one_cos, -one_sin], axis=2).reshape(piece_rows, 2 * devices, devices)
        result = jnp.einsum(
            "skr,rsbc->ksbc", table_one, columns, preferred_element_type=jnp.float32
        )
        section_one.append(result.astype(jnp.bfloat16).reshape(devices, 2, piece_rows, 3, channels))
    section_one = regroup_blocks(jnp.stack(section_one, axis=2))
    full_sample = anchor[:, None] * piece_rows + local_steps[None, :]
    step_cos, step_sin = rounded_trig(
        full_sample[:, :, None] * step_index[None, None, :], tokens_here
    )
    real_col = jnp.stack([step_cos, step_sin])
    imag_col = jnp.stack([-step_sin, step_cos])
    table_two = jnp.stack([real_col, imag_col], axis=3)
    section_three = []
    for half in range(2):
        spectra = jnp.einsum(
            "oisbc,iosjk->jkbc",
            section_one[:, :, half],
            table_two,
            preferred_element_type=jnp.float32,
        )
        spec_real, spec_imag = (spectra[0], spectra[1])
        value_real, gate_real, filter_real = (spec_real[:, 0], spec_real[:, 1], spec_real[:, 2])
        value_imag, gate_imag, filter_imag = (spec_imag[:, 0], spec_imag[:, 1], spec_imag[:, 2])
        forward_real = value_real * filter_real - value_imag * filter_imag
        forward_imag = value_real * filter_imag + value_imag * filter_real
        backward_real = filter_real * gate_real + filter_imag * gate_imag
        backward_imag = filter_real * gate_imag - filter_imag * gate_real
        lag_real = (value_real * gate_real + value_imag * gate_imag) * factor
        lag_imag = (value_real * gate_imag - value_imag * gate_real) * factor
        products = jnp.stack(
            [
                jnp.stack([forward_real, backward_real, lag_real], axis=1),
                jnp.stack([forward_imag, backward_imag, lag_imag], axis=1),
            ]
        ).astype(jnp.bfloat16)
        freq_held = half * devices + position
        phase_three = (
            step_index[None, :] * step_index[:, None] * radix_count
            + step_index[None, :] * freq_held
        )
        three_cos, three_sin = rounded_trig(phase_three, points)
        real_row = jnp.stack([three_cos, -three_sin])
        imag_row = jnp.stack([three_sin, three_cos])
        table_three = jnp.stack([real_row, imag_row], axis=2)
        result = jnp.einsum(
            "ikbc,ikjs->sjbc", products, table_three, preferred_element_type=jnp.float32
        )
        section_three.append(result.astype(jnp.bfloat16))
    section_three = jnp.stack(section_three, axis=2).reshape(devices, piece_rows, 2, 2, 3, channels)
    rows_back = regroup_blocks(section_three)
    freq_last = halves[:, None] * devices + anchor[None, :]
    last_cos, last_sin = rounded_trig(anchor[None, None, :] * freq_last[:, :, None], radix_count)
    table_four = jnp.stack([last_cos, -last_sin])
    restored = (
        jnp.einsum("opjhbc,jhor->rpbc", rows_back, table_four, preferred_element_type=jnp.float32)
        / points
    )
    home_rows = regroup_blocks(restored.astype(jnp.bfloat16)).reshape(tokens_here, 3, channels)
    convolved = home_rows[:, 0].astype(jnp.float32)
    correlated = home_rows[:, 1].astype(jnp.float32)
    filter_grad = home_rows[:, 2]
    product_full = product.astype(jnp.float32)
    mixing = convolved + skip_gain[None, :] * product_full
    layer_out = (query_rows.astype(jnp.float32) * mixing).astype(jnp.bfloat16)
    query_grad = (out_grad.astype(jnp.float32) * mixing).astype(jnp.bfloat16)
    carried = correlated + skip_gain[None, :] * gate_grad
    key_grad = (carried * value_rows.astype(jnp.float32)).astype(jnp.bfloat16)
    value_grad = (carried * key_rows.astype(jnp.float32)).astype(jnp.bfloat16)
    skip_part = jnp.sum(gate_grad * product_full, axis=0)
    skip_sum = lax.psum(skip_part, ("outer", "inner"))
    return (layer_out, query_grad, key_grad, value_grad, filter_grad, skip_sum * factor)


def body(*arrays):
    lanes_full = arrays[0].shape[1] == lax.axis_size(AXES) * LANES
    return (channel_body if lanes_full else frequency_body)(*arrays)


def solution(mesh):
    return jax.shard_map(
        body,
        mesh=mesh,
        in_specs=(
            P(("outer", "inner"), None),
            P(("outer", "inner"), None),
            P(("outer", "inner"), None),
            P(("outer", "inner"), None),
            P(("outer", "inner"), None),
            P(),
        ),
        out_specs=(
            P(("outer", "inner"), None),
            P(("outer", "inner"), None),
            P(("outer", "inner"), None),
            P(("outer", "inner"), None),
            P(("outer", "inner"), None),
            P(),
        ),
        check_vma=False,
    )
```

```python
import functools
import math

import jax
import jax.numpy as jnp
import ml_dtypes
import numpy as np
from jax import lax
from jax.experimental import pallas as pl
from jax.experimental.pallas import tpu as pltpu
from jax.sharding import PartitionSpec as P

TWO_PI = 2.0 * math.pi
AXES = ("outer", "inner")
LANES = 128
SUBLANES = 8
GROUPS = 4
SPARE = SUBLANES
BF16 = jnp.bfloat16
F32 = jnp.float32


def table_trig(phase, modulus):
    angle = (phase % modulus).astype(np.float32) * np.float32(TWO_PI / modulus)
    return tuple(
        part.astype(ml_dtypes.bfloat16).astype(np.float32) for part in (np.cos(angle), np.sin(angle))
    )


def make_tables(rows, steps):
    planes = rows + 1
    points = 2 * rows * steps
    row = np.arange(rows)
    plane = np.arange(planes)
    step = np.arange(steps)
    eye = np.eye(SUBLANES, dtype=np.float32)
    phase = row[None, None, :] * plane[None, :, None] * steps + step[:, None, None] * plane[None, :, None]
    cos, sin = table_trig(phase, points)
    first = np.stack([cos, -sin], axis=1).reshape(steps // SUBLANES, SUBLANES, 2, planes, rows)
    first = np.einsum("bipkr,ij->bpkirj", first, eye)
    first = first.reshape(steps // SUBLANES, 2 * planes * SUBLANES, rows * SUBLANES)
    cos, sin = table_trig(step[:, None] * step[None, :], steps)
    second = np.block([[cos, sin], [-sin, cos]])
    phase = step[None, :, None] * step[None, None, :] * (2 * rows) + step[None, :, None] * plane[:, None, None]
    cos, sin = table_trig(phase, points)
    third = np.concatenate(
        [np.concatenate([cos, -sin], axis=2), np.concatenate([sin, cos], axis=2)], axis=1
    )
    cos, sin = table_trig(row[:, None] * plane[None, :], 2 * rows)
    weight = np.where((plane == 0) | (plane == rows), 1.0, 2.0).astype(np.float32)
    last = np.stack([cos * weight, -sin * weight], axis=1)
    last = np.einsum("rpk,ij->ripkj", last, eye).reshape(rows * SUBLANES, 2 * planes * SUBLANES)
    return tuple(table.astype(ml_dtypes.bfloat16) for table in (first, second, third, last))


def dot(a, b):
    return jnp.dot(a, b, preferred_element_type=F32)


def product_of(key, value):
    return (key.astype(F32) * value.astype(F32)).astype(BF16)


def row_group(b, size=2 * SUBLANES):
    return pl.ds(pl.multiple_of(b * size, size), size)


def pack_kernel(filter_ref, key_ref, value_ref, out_ref, held, made, arrived, left):
    tokens, groups = filter_ref.shape[0], arrived.shape[1]
    blocks = out_ref.shape[0] // groups
    sources = (filter_ref, key_ref, value_ref)

    def copies_in(g):
        cols = pl.ds(g * blocks * LANES, blocks * LANES)
        return [pltpu.make_async_copy(ref.at[:, cols], held.at[i, :, cols], arrived.at[i, g]) for i, ref in enumerate(sources)]

    def copy_out(g):
        some = pl.ds(g * blocks, blocks)
        return pltpu.make_async_copy(made.at[some], out_ref.at[some], left.at[g])

    for g in range(groups):
        for copy in copies_in(g):
            copy.start()
    for g in range(groups):
        for copy in copies_in(g):
            copy.wait()
        for d in range(g * blocks, (g + 1) * blocks):
            cols = pl.ds(d * LANES, LANES)
            made[d, :tokens, :] = held[0, :, cols]
            made[d, tokens:, :] = product_of(held[1, :, cols], held[2, :, cols])
        copy_out(g).start()
    for g in range(groups):
        copy_out(g).wait()


def gate_kernel(query_ref, grad_ref, out_ref):
    for d in range(out_ref.shape[0]):
        cols = pl.ds(d * LANES, LANES)
        out_ref[d] = (grad_ref[:, cols].astype(F32) * query_ref[:, cols].astype(F32)).astype(BF16)


def looped(count, chunk, one):
    def several(i, _):
        for j in range(chunk):
            one(i * chunk + j)
        return 0

    lax.fori_loop(0, count // chunk, several, 0)
    for i in range(count - count % chunk, count):
        one(i)


def spectrum_of(read, first_ref, second_ref, section, store):
    planes, steps, width = section.shape[0], section.shape[1] // 2, section.shape[2]

    def one(b):
        pair = read(b)
        for half in range(2):
            block = pair[:, half * SUBLANES : (half + 1) * SUBLANES, :]
            result = dot(first_ref[2 * b + half], block.reshape(-1, width).astype(BF16))
            result = result.reshape(2, planes, SUBLANES, width)
            section[:, row_group(2 * b + half, SUBLANES), :] = result[0]
            section[:, row_group(2 * b + half + steps // SUBLANES, SUBLANES), :] = result[1]

    looped(steps // (2 * SUBLANES), 2, one)

    def two(k):
        store(k, dot(second_ref[...], section[k].astype(BF16)))

    looped(planes, 8, two)


def inverse_of(product_at, third_ref, last_ref, section, scale, write):
    planes, steps, width = section.shape[0], section.shape[1] // 2, section.shape[2]

    def three(k):
        section[k] = dot(third_ref[k], product_at(k))

    looped(planes, 8, three)

    def four(b):
        halves = []
        for half in range(2):
            real = section[:, row_group(2 * b + half, SUBLANES), :].reshape(-1, width)
            imag = section[:, row_group(2 * b + half + steps // SUBLANES, SUBLANES), :].reshape(-1, width)
            flat = jnp.concatenate([real, imag], axis=0).astype(BF16)
            halves.append((dot(last_ref[...], flat) * scale).reshape(-1, SUBLANES, width))
        write(b, jnp.concatenate(halves, axis=1).astype(BF16))

    looped(steps // (2 * SUBLANES), 2, four)


def parts_of(plane):
    steps = plane.shape[0] // 2
    return plane[:steps], plane[steps:]


def conj_product(a, b):
    (ar, ai), (br, bi) = parts_of(a), parts_of(b)
    return jnp.concatenate([ar * br + ai * bi, ar * bi - ai * br], axis=0)


def forward_kernel(scale, packed_ref, first_ref, second_ref, third_ref, last_ref, out_ref, spectra_ref, wide, narrow):
    pairs = packed_ref.shape[1] // (4 * SUBLANES)

    def read(b):
        filt, value = packed_ref[:, row_group(b), :], packed_ref[:, row_group(b + pairs), :]
        return jnp.concatenate([filt.astype(F32), value.astype(F32)], axis=2)

    def store(k, plane):
        spectra_ref[k] = plane

    spectrum_of(read, first_ref, second_ref, wide, store)

    def product_at(k):
        (fr, fi), (vr, vi) = parts_of(spectra_ref[k, :, :LANES]), parts_of(spectra_ref[k, :, LANES:])
        return jnp.concatenate([vr * fr - vi * fi, vr * fi + vi * fr], axis=0).astype(BF16)

    def write(b, rows):
        out_ref[:, row_group(b), :] = rows

    inverse_of(product_at, third_ref, last_ref, narrow, scale, write)


def split_rows(total):
    rows = []
    for _ in range(3):
        rows.append(total.astype(BF16).astype(F32))
        total = total - rows[-1]
    rows.append(jnp.zeros((SPARE - len(rows), total.shape[1]), F32))
    return jnp.concatenate(rows, axis=0).astype(BF16)


def backward_kernel(scale, factor, gate_ref, packed_ref, spectra_ref, first_ref, second_ref, third_ref, last_ref, out_ref, section, gate_spectrum, wide):
    steps = gate_ref.shape[1]
    pairs = steps // (2 * SUBLANES)

    def gate_times_product(d, total):
        return total + gate_ref[d].astype(F32) * packed_ref[d, steps:, :].astype(F32)

    total = lax.fori_loop(0, gate_ref.shape[0], gate_times_product, jnp.zeros((steps, LANES), F32))
    spare = split_rows(jnp.sum(total, axis=0, keepdims=True) * factor)
    for d in range(out_ref.shape[0]):
        out_ref[d, 2 * steps :, :] = spare

    def read(b):
        return gate_ref[:, row_group(b), :].astype(F32)

    def store(k, plane):
        gate_spectrum[k] = plane

    spectrum_of(read, first_ref, second_ref, section, store)

    def product_at(k):
        gate = gate_spectrum[k]
        back = conj_product(spectra_ref[k, :, :LANES], gate)
        lag = conj_product(spectra_ref[k, :, LANES:], gate) * factor
        return jnp.concatenate([back, lag], axis=1).astype(BF16)

    def write(b, rows):
        out_ref[:, row_group(b), :] = rows[:, :, :LANES]
        out_ref[:, row_group(b + pairs), :] = rows[:, :, LANES:]

    inverse_of(product_at, third_ref, last_ref, wide, scale, write)


def mixing_kernel(conv_ref, query_ref, grad_ref, key_ref, value_ref, gain_ref, layer_ref, query_grad_ref):
    blocks = layer_ref.shape[1] // LANES
    for d in range(blocks):
        cols = pl.ds(d * LANES, LANES)
        query, grad, gain = query_ref[:, cols].astype(F32), grad_ref[:, cols].astype(F32), gain_ref[:, cols]
        product = product_of(key_ref[:, cols], value_ref[:, cols]).astype(F32)
        mixing = conv_ref[pl.program_id(0) * blocks + d].astype(F32) + gain * product
        layer_ref[:, cols] = (query * mixing).astype(BF16)
        query_grad_ref[:, cols] = (grad * mixing).astype(BF16)


def carried_kernel(back_ref, query_ref, grad_ref, key_ref, value_ref, gain_ref, *refs):
    *row_refs, skip_ref, back, held, made, arrived, left = refs
    branches = (query_ref, grad_ref, key_ref, value_ref)
    tokens, groups = key_ref.shape[0], arrived.shape[1]
    blocks = back_ref.shape[0] // groups

    def copies_in(g):
        some, cols = pl.ds(g * blocks, blocks), pl.ds(g * blocks * LANES, blocks * LANES)
        pairs = [(ref.at[:, cols], held.at[i, :, cols]) for i, ref in enumerate(branches)]
        pairs.append((back_ref.at[some], back.at[some]))
        return [pltpu.make_async_copy(a, b, arrived.at[i, g]) for i, (a, b) in enumerate(pairs)]

    def copies_out(g):
        cols = pl.ds(g * blocks * LANES, blocks * LANES)
        return [pltpu.make_async_copy(made.at[i, :, cols], ref.at[:, cols], left.at[i, g]) for i, ref in enumerate(row_refs)]

    for g in range(groups):
        for copy in copies_in(g):
            copy.start()
    for g in range(groups):
        for copy in copies_in(g):
            copy.wait()
        for d in range(g * blocks, (g + 1) * blocks):
            cols = pl.ds(d * LANES, LANES)
            query, grad, key, value = (held[i, :, cols].astype(F32) for i in range(len(branches)))
            carried = back[d, :tokens, :].astype(F32) + gain_ref[:, cols] * (grad * query)
            made[0, :, cols] = (carried * value).astype(BF16)
            made[1, :, cols] = (carried * key).astype(BF16)
            made[2, :, cols] = back[d, tokens : 2 * tokens, :]
            skip_ref[:, cols] = jnp.sum(back[d, 2 * tokens :, :].astype(F32), axis=0, keepdims=True)
        for copy in copies_out(g):
            copy.start()
    for g in range(groups):
        for copy in copies_out(g):
            copy.wait()


def exchange(blocks):
    return lax.all_to_all(blocks, AXES, split_axis=0, concat_axis=0, tiled=True)


def limit(mib):
    return pltpu.CompilerParams(vmem_limit_bytes=mib * 1024 * 1024)


def kernel(body, *arrays, after=(), in_specs=None, **options):
    count, waits = len(arrays), len(after)

    def waiting(*refs):
        body(*refs[:count], *refs[count + waits :])

    specs = list(in_specs or [pl.BlockSpec()] * count) + [pl.BlockSpec(memory_space=pl.ANY)] * waits
    return pl.pallas_call(waiting, in_specs=specs, **options)(*arrays, *after)


def channel_body(query_rows, key_rows, value_rows, out_grad, filter_rows, skip_gain):
    devices = lax.axis_size(AXES)
    tokens, channels = query_rows.shape
    length = tokens * devices
    factor = 1.0 / math.sqrt(length)
    scale = 1.0 / (2 * length)
    planes = devices + 1
    tables = [jnp.asarray(table) for table in make_tables(devices, tokens)]
    blocks = math.gcd(devices, 8)
    grid = (devices // blocks,)
    back_rows = 2 * tokens + SPARE
    rows_spec = pl.BlockSpec((tokens, blocks * LANES), lambda i: (0, i))
    vector_spec = pl.BlockSpec((1, blocks * LANES), lambda i: (0, i))
    single_spec = pl.BlockSpec((blocks, tokens, LANES), lambda i: (i, 0, 0))
    rows_shape = jax.ShapeDtypeStruct((tokens, channels), BF16)
    single_shape = jax.ShapeDtypeStruct((devices, tokens, LANES), BF16)
    double_shape = jax.ShapeDtypeStruct((devices, 2 * tokens, LANES), BF16)
    back_shape = jax.ShapeDtypeStruct((devices, back_rows, LANES), BF16)
    narrow = pltpu.VMEM((planes, 2 * tokens, LANES), F32)
    wide = pltpu.VMEM((planes, 2 * tokens, 2 * LANES), F32)

    in_hbm = pl.BlockSpec(memory_space=pltpu.HBM)
    groups = math.gcd(devices, GROUPS)
    packed = kernel(
        pack_kernel, filter_rows, key_rows, value_rows, in_specs=[in_hbm] * 3, out_specs=in_hbm,
        out_shape=double_shape, compiler_params=limit(56),
        scratch_shapes=[
            pltpu.VMEM((3, tokens, channels), BF16), pltpu.VMEM((devices, 2 * tokens, LANES), BF16),
            pltpu.SemaphoreType.DMA((3, groups)), pltpu.SemaphoreType.DMA((groups,)),
        ],
    )
    gate = kernel(
        gate_kernel, query_rows, out_grad, after=[packed], grid=grid,
        in_specs=[rows_spec] * 2, out_specs=single_spec, out_shape=single_shape,
    )
    packed = exchange(packed)
    gate = exchange(gate)
    convolved, spectra = kernel(
        functools.partial(forward_kernel, scale), packed, *tables,
        out_shape=[single_shape, jax.ShapeDtypeStruct((planes, 2 * tokens, 2 * LANES), F32)],
        scratch_shapes=[wide, narrow], compiler_params=limit(48),
    )
    convolved = exchange(convolved)
    back = kernel(
        functools.partial(backward_kernel, scale, factor), gate, packed, spectra, *tables,
        out_shape=back_shape, scratch_shapes=[narrow, narrow, wide], compiler_params=limit(52),
    )
    back = exchange(back)
    whole = pl.BlockSpec(memory_space=pltpu.VMEM)
    branches = (query_rows, out_grad, key_rows, value_rows)
    gain = skip_gain[None, :]
    layer_out, query_grad = kernel(
        mixing_kernel, convolved, *branches, gain, grid=grid, in_specs=[whole] + [rows_spec] * 4 + [vector_spec],
        out_specs=[rows_spec] * 2, out_shape=[rows_shape] * 2, compiler_params=limit(24),
    )
    key_grad, value_grad, filter_grad, skip_grad = kernel(
        carried_kernel, back, *branches, gain, in_specs=[in_hbm] * 5 + [pl.BlockSpec()],
        out_specs=[in_hbm] * 3 + [pl.BlockSpec()],
        out_shape=[rows_shape] * 3 + [jax.ShapeDtypeStruct((1, channels), F32)], compiler_params=limit(24),
        scratch_shapes=[
            pltpu.VMEM((devices, back_rows, LANES), BF16), pltpu.VMEM((4, tokens, channels), BF16),
            pltpu.VMEM((3, tokens, channels), BF16),
            pltpu.SemaphoreType.DMA((5, groups)), pltpu.SemaphoreType.DMA((3, groups)),
        ],
    )
    return (layer_out, query_grad, key_grad, value_grad, filter_grad, skip_grad[0])


def rounded_trig(phase, modulus):
    angle = (phase % modulus).astype(jnp.float32) * (TWO_PI / modulus)
    return (jnp.cos(angle).astype(jnp.bfloat16), jnp.sin(angle).astype(jnp.bfloat16))


def regroup_blocks(blocks):
    return lax.all_to_all(blocks, ("outer", "inner"), split_axis=0, concat_axis=0, tiled=True)


def frequency_body(query_rows, key_rows, value_rows, out_grad, filter_rows, skip_gain):
    devices = lax.axis_size(("outer", "inner"))
    position = lax.axis_index(("outer", "inner"))
    tokens_here = query_rows.shape[0]
    channels = query_rows.shape[1]
    piece_rows = tokens_here // devices
    length = tokens_here * devices
    points = 2 * length
    radix_count = 2 * devices
    factor = 1.0 / math.sqrt(length)
    product = (key_rows.astype(jnp.float32) * value_rows.astype(jnp.float32)).astype(jnp.bfloat16)
    gate_grad = out_grad.astype(jnp.float32) * query_rows.astype(jnp.float32)
    signals = jnp.stack([product, gate_grad.astype(jnp.bfloat16), filter_rows], axis=1)
    columns = regroup_blocks(signals.reshape(devices, piece_rows, 3, channels))
    anchor = jnp.arange(devices, dtype=jnp.int32)
    halves = jnp.arange(2, dtype=jnp.int32)
    local_steps = jnp.arange(piece_rows, dtype=jnp.int32)
    step_index = jnp.arange(tokens_here, dtype=jnp.int32)
    sample = position * piece_rows + local_steps
    section_one = []
    for half in range(2):
        freq_one = half * devices + anchor
        phase = (
            anchor[None, None, :] * freq_one[None, :, None] * tokens_here
            + sample[:, None, None] * freq_one[None, :, None]
        )
        one_cos, one_sin = rounded_trig(phase, points)
        table_one = jnp.stack([one_cos, -one_sin], axis=2).reshape(piece_rows, 2 * devices, devices)
        result = jnp.einsum(
            "skr,rsbc->ksbc", table_one, columns, preferred_element_type=jnp.float32
        )
        section_one.append(result.astype(jnp.bfloat16).reshape(devices, 2, piece_rows, 3, channels))
    section_one = regroup_blocks(jnp.stack(section_one, axis=2))
    full_sample = anchor[:, None] * piece_rows + local_steps[None, :]
    step_cos, step_sin = rounded_trig(
        full_sample[:, :, None] * step_index[None, None, :], tokens_here
    )
    real_col = jnp.stack([step_cos, step_sin])
    imag_col = jnp.stack([-step_sin, step_cos])
    table_two = jnp.stack([real_col, imag_col], axis=3)
    section_three = []
    for half in range(2):
        spectra = jnp.einsum(
            "oisbc,iosjk->jkbc",
            section_one[:, :, half],
            table_two,
            preferred_element_type=jnp.float32,
        )
        spec_real, spec_imag = (spectra[0], spectra[1])
        value_real, gate_real, filter_real = (spec_real[:, 0], spec_real[:, 1], spec_real[:, 2])
        value_imag, gate_imag, filter_imag = (spec_imag[:, 0], spec_imag[:, 1], spec_imag[:, 2])
        forward_real = value_real * filter_real - value_imag * filter_imag
        forward_imag = value_real * filter_imag + value_imag * filter_real
        backward_real = filter_real * gate_real + filter_imag * gate_imag
        backward_imag = filter_real * gate_imag - filter_imag * gate_real
        lag_real = (value_real * gate_real + value_imag * gate_imag) * factor
        lag_imag = (value_real * gate_imag - value_imag * gate_real) * factor
        products = jnp.stack(
            [
                jnp.stack([forward_real, backward_real, lag_real], axis=1),
                jnp.stack([forward_imag, backward_imag, lag_imag], axis=1),
            ]
        ).astype(jnp.bfloat16)
        freq_held = half * devices + position
        phase_three = (
            step_index[None, :] * step_index[:, None] * radix_count
            + step_index[None, :] * freq_held
        )
        three_cos, three_sin = rounded_trig(phase_three, points)
        real_row = jnp.stack([three_cos, -three_sin])
        imag_row = jnp.stack([three_sin, three_cos])
        table_three = jnp.stack([real_row, imag_row], axis=2)
        result = jnp.einsum(
            "ikbc,ikjs->sjbc", products, table_three, preferred_element_type=jnp.float32
        )
        section_three.append(result.astype(jnp.bfloat16))
    section_three = jnp.stack(section_three, axis=2).reshape(devices, piece_rows, 2, 2, 3, channels)
    rows_back = regroup_blocks(section_three)
    freq_last = halves[:, None] * devices + anchor[None, :]
    last_cos, last_sin = rounded_trig(anchor[None, None, :] * freq_last[:, :, None], radix_count)
    table_four = jnp.stack([last_cos, -last_sin])
    restored = (
        jnp.einsum("opjhbc,jhor->rpbc", rows_back, table_four, preferred_element_type=jnp.float32)
        / points
    )
    home_rows = regroup_blocks(restored.astype(jnp.bfloat16)).reshape(tokens_here, 3, channels)
    convolved = home_rows[:, 0].astype(jnp.float32)
    correlated = home_rows[:, 1].astype(jnp.float32)
    filter_grad = home_rows[:, 2]
    product_full = product.astype(jnp.float32)
    mixing = convolved + skip_gain[None, :] * product_full
    layer_out = (query_rows.astype(jnp.float32) * mixing).astype(jnp.bfloat16)
    query_grad = (out_grad.astype(jnp.float32) * mixing).astype(jnp.bfloat16)
    carried = correlated + skip_gain[None, :] * gate_grad
    key_grad = (carried * value_rows.astype(jnp.float32)).astype(jnp.bfloat16)
    value_grad = (carried * key_rows.astype(jnp.float32)).astype(jnp.bfloat16)
    skip_part = jnp.sum(gate_grad * product_full, axis=0)
    skip_sum = lax.psum(skip_part, ("outer", "inner"))
    return (layer_out, query_grad, key_grad, value_grad, filter_grad, skip_sum * factor)


def body(*arrays):
    lanes_full = arrays[0].shape[1] == lax.axis_size(AXES) * LANES
    return (channel_body if lanes_full else frequency_body)(*arrays)


def solution(mesh):
    return jax.shard_map(
        body,
        mesh=mesh,
        in_specs=(
            P(("outer", "inner"), None),
            P(("outer", "inner"), None),
            P(("outer", "inner"), None),
            P(("outer", "inner"), None),
            P(("outer", "inner"), None),
            P(),
        ),
        out_specs=(
            P(("outer", "inner"), None),
            P(("outer", "inner"), None),
            P(("outer", "inner"), None),
            P(("outer", "inner"), None),
            P(("outer", "inner"), None),
            P(),
        ),
        check_vma=False,
    )
```

```python
import functools
import math

import jax
import jax.numpy as jnp
import ml_dtypes
import numpy as np
from jax import lax
from jax.experimental import pallas as pl
from jax.experimental.pallas import tpu as pltpu
from jax.sharding import PartitionSpec as P

TWO_PI = 2.0 * math.pi
AXES = ("outer", "inner")
LANES = 128
SUBLANES = 8
GROUPS = 4
SPARE = 2 * SUBLANES
BF16 = jnp.bfloat16
F32 = jnp.float32


def table_trig(phase, modulus):
    angle = (phase % modulus).astype(np.float32) * np.float32(TWO_PI / modulus)
    return tuple(
        part.astype(ml_dtypes.bfloat16).astype(np.float32) for part in (np.cos(angle), np.sin(angle))
    )


def make_tables(rows, steps):
    planes = rows + 1
    points = 2 * rows * steps
    row = np.arange(rows)
    plane = np.arange(planes)
    step = np.arange(steps)
    eye = np.eye(SUBLANES, dtype=np.float32)
    phase = row[None, None, :] * plane[None, :, None] * steps + step[:, None, None] * plane[None, :, None]
    cos, sin = table_trig(phase, points)
    first = np.stack([cos, -sin], axis=1).reshape(steps // SUBLANES, SUBLANES, 2, planes, rows)
    first = np.einsum("bipkr,ij->bpkirj", first, eye)
    first = first.reshape(steps // SUBLANES, 2 * planes * SUBLANES, rows * SUBLANES)
    cos, sin = table_trig(step[:, None] * step[None, :], steps)
    second = np.block([[cos, sin], [-sin, cos]])
    phase = step[None, :, None] * step[None, None, :] * (2 * rows) + step[None, :, None] * plane[:, None, None]
    cos, sin = table_trig(phase, points)
    third = np.concatenate(
        [np.concatenate([cos, -sin], axis=2), np.concatenate([sin, cos], axis=2)], axis=1
    )
    cos, sin = table_trig(row[:, None] * plane[None, :], 2 * rows)
    weight = np.where((plane == 0) | (plane == rows), 1.0, 2.0).astype(np.float32)
    last = np.stack([cos * weight, -sin * weight], axis=1)
    last = np.einsum("rpk,ij->ripkj", last, eye).reshape(rows * SUBLANES, 2 * planes * SUBLANES)
    return tuple(table.astype(ml_dtypes.bfloat16) for table in (first, second, third, last))


def dot(a, b):
    return jnp.dot(a, b, preferred_element_type=F32)


def product_of(key, value):
    return (key.astype(F32) * value.astype(F32)).astype(BF16)


def row_group(b, size=2 * SUBLANES):
    return pl.ds(pl.multiple_of(b * size, size), size)


def pack_kernel(filter_ref, key_ref, value_ref, out_ref, held, made, arrived, left):
    tokens, groups = filter_ref.shape[0], arrived.shape[1]
    blocks = out_ref.shape[0] // groups
    sources = (filter_ref, key_ref, value_ref)

    def copies_in(g):
        cols = pl.ds(g * blocks * LANES, blocks * LANES)
        return [pltpu.make_async_copy(ref.at[:, cols], held.at[i, :, cols], arrived.at[i, g]) for i, ref in enumerate(sources)]

    def copy_out(g):
        some = pl.ds(g * blocks, blocks)
        return pltpu.make_async_copy(made.at[some], out_ref.at[some], left.at[g])

    for g in range(groups):
        for copy in copies_in(g):
            copy.start()
    for g in range(groups):
        for copy in copies_in(g):
            copy.wait()
        for d in range(g * blocks, (g + 1) * blocks):
            cols = pl.ds(d * LANES, LANES)
            made[d, :tokens, :] = held[0, :, cols]
            made[d, tokens:, :] = product_of(held[1, :, cols], held[2, :, cols])
        copy_out(g).start()
    for g in range(groups):
        copy_out(g).wait()


def gate_kernel(query_ref, grad_ref, out_ref):
    for d in range(out_ref.shape[0]):
        cols = pl.ds(d * LANES, LANES)
        out_ref[d] = (grad_ref[:, cols].astype(F32) * query_ref[:, cols].astype(F32)).astype(BF16)


def looped(count, chunk, one):
    def several(i, _):
        for j in range(chunk):
            one(i * chunk + j)
        return 0

    lax.fori_loop(0, count // chunk, several, 0)
    for i in range(count - count % chunk, count):
        one(i)


def spectrum_of(read, first_ref, second_ref, section, store):
    planes, steps, width = section.shape[0], section.shape[1] // 2, section.shape[2]

    def one(b):
        pair = read(b)
        for half in range(2):
            block = pair[:, half * SUBLANES : (half + 1) * SUBLANES, :]
            result = dot(first_ref[2 * b + half], block.reshape(-1, width).astype(BF16))
            result = result.reshape(2, planes, SUBLANES, width)
            section[:, row_group(2 * b + half, SUBLANES), :] = result[0]
            section[:, row_group(2 * b + half + steps // SUBLANES, SUBLANES), :] = result[1]

    looped(steps // (2 * SUBLANES), 2, one)

    def two(k):
        store(k, dot(second_ref[...], section[k].astype(BF16)))

    looped(planes, 8, two)


def inverse_of(product_at, third_ref, last_ref, section, scale, write):
    planes, steps, width = section.shape[0], section.shape[1] // 2, section.shape[2]

    def three(k):
        section[k] = dot(third_ref[k], product_at(k))

    looped(planes, 8, three)

    def four(b):
        halves = []
        for half in range(2):
            real = section[:, row_group(2 * b + half, SUBLANES), :].reshape(-1, width)
            imag = section[:, row_group(2 * b + half + steps // SUBLANES, SUBLANES), :].reshape(-1, width)
            flat = jnp.concatenate([real, imag], axis=0).astype(BF16)
            halves.append((dot(last_ref[...], flat) * scale).reshape(-1, SUBLANES, width))
        write(b, jnp.concatenate(halves, axis=1).astype(BF16))

    looped(steps // (2 * SUBLANES), 2, four)


def parts_of(plane):
    steps = plane.shape[0] // 2
    return plane[:steps], plane[steps:]


def conj_product(a, b):
    (ar, ai), (br, bi) = parts_of(a), parts_of(b)
    return jnp.concatenate([ar * br + ai * bi, ar * bi - ai * br], axis=0)


def forward_kernel(scale, packed_ref, first_ref, second_ref, third_ref, last_ref, out_ref, spectra_ref, wide, narrow):
    pairs = packed_ref.shape[1] // (4 * SUBLANES)

    def read(b):
        filt, value = packed_ref[:, row_group(b), :], packed_ref[:, row_group(b + pairs), :]
        return jnp.concatenate([filt.astype(F32), value.astype(F32)], axis=2)

    def store(k, plane):
        spectra_ref[k] = plane

    spectrum_of(read, first_ref, second_ref, wide, store)

    def product_at(k):
        (fr, fi), (vr, vi) = parts_of(spectra_ref[k, :, :LANES]), parts_of(spectra_ref[k, :, LANES:])
        return jnp.concatenate([vr * fr - vi * fi, vr * fi + vi * fr], axis=0).astype(BF16)

    def write(b, rows):
        out_ref[:, row_group(b), :] = rows

    inverse_of(product_at, third_ref, last_ref, narrow, scale, write)


def split_rows(total):
    rows = []
    for _ in range(3):
        rows.append(total.astype(BF16).astype(F32))
        total = total - rows[-1]
    rows.append(jnp.zeros((SPARE - len(rows), total.shape[1]), F32))
    return jnp.concatenate(rows, axis=0).astype(BF16)


def backward_kernel(scale, factor, gate_ref, packed_ref, spectra_ref, first_ref, second_ref, third_ref, last_ref, out_ref, section, gate_spectrum, wide):
    steps = gate_ref.shape[1]
    pairs = steps // (2 * SUBLANES)

    def gate_times_product(d, total):
        return total + gate_ref[d].astype(F32) * packed_ref[d, steps:, :].astype(F32)

    total = lax.fori_loop(0, gate_ref.shape[0], gate_times_product, jnp.zeros((steps, LANES), F32))
    spare = split_rows(jnp.sum(total, axis=0, keepdims=True) * factor)
    for d in range(out_ref.shape[0]):
        out_ref[d, 2 * steps :, :] = spare

    def read(b):
        return gate_ref[:, row_group(b), :].astype(F32)

    def store(k, plane):
        gate_spectrum[k] = plane

    spectrum_of(read, first_ref, second_ref, section, store)

    def product_at(k):
        gate = gate_spectrum[k]
        back = conj_product(spectra_ref[k, :, :LANES], gate)
        lag = conj_product(spectra_ref[k, :, LANES:], gate) * factor
        return jnp.concatenate([back, lag], axis=1).astype(BF16)

    def write(b, rows):
        out_ref[:, row_group(b), :] = rows[:, :, :LANES]
        out_ref[:, row_group(b + pairs), :] = rows[:, :, LANES:]

    inverse_of(product_at, third_ref, last_ref, wide, scale, write)


def mixing_kernel(conv_ref, query_ref, grad_ref, key_ref, value_ref, gain_ref, layer_ref, query_grad_ref):
    blocks = layer_ref.shape[1] // LANES
    for d in range(blocks):
        cols = pl.ds(d * LANES, LANES)
        query, grad, gain = query_ref[:, cols].astype(F32), grad_ref[:, cols].astype(F32), gain_ref[:, cols]
        product = product_of(key_ref[:, cols], value_ref[:, cols]).astype(F32)
        mixing = conv_ref[pl.program_id(0) * blocks + d].astype(F32) + gain * product
        layer_ref[:, cols] = (query * mixing).astype(BF16)
        query_grad_ref[:, cols] = (grad * mixing).astype(BF16)


def carried_kernel(back_ref, query_ref, grad_ref, key_ref, value_ref, gain_ref, *refs):
    *row_refs, skip_ref, back, made, arrived, left = refs
    tokens, groups = key_ref.shape[0], arrived.shape[0]
    blocks = back_ref.shape[0] // groups

    def copy_in(g):
        some = pl.ds(g * blocks, blocks)
        return pltpu.make_async_copy(back_ref.at[some], back.at[some], arrived.at[g])

    def copies_out(g):
        cols = pl.ds(g * blocks * LANES, blocks * LANES)
        return [pltpu.make_async_copy(made.at[i, :, cols], ref.at[:, cols], left.at[i, g]) for i, ref in enumerate(row_refs)]

    for g in range(groups):
        copy_in(g).start()
    for g in range(groups):
        copy_in(g).wait()
        for d in range(g * blocks, (g + 1) * blocks):
            cols = pl.ds(d * LANES, LANES)
            gate = grad_ref[:, cols].astype(F32) * query_ref[:, cols].astype(F32)
            carried = back[d, :tokens, :].astype(F32) + gain_ref[:, cols] * gate
            made[0, :, cols] = (carried * value_ref[:, cols].astype(F32)).astype(BF16)
            made[1, :, cols] = (carried * key_ref[:, cols].astype(F32)).astype(BF16)
            made[2, :, cols] = back[d, tokens : 2 * tokens, :]
            skip_ref[:, cols] = jnp.sum(back[d, 2 * tokens :, :].astype(F32), axis=0, keepdims=True)
        for copy in copies_out(g):
            copy.start()
    for g in range(groups):
        for copy in copies_out(g):
            copy.wait()


def exchange(blocks):
    return lax.all_to_all(blocks, AXES, split_axis=0, concat_axis=0, tiled=True)


def limit(mib):
    return pltpu.CompilerParams(vmem_limit_bytes=mib * 1024 * 1024)


def kernel(body, *arrays, after=(), in_specs=None, **options):
    count, waits = len(arrays), len(after)

    def waiting(*refs):
        body(*refs[:count], *refs[count + waits :])

    specs = list(in_specs or [pl.BlockSpec()] * count) + [pl.BlockSpec(memory_space=pl.ANY)] * waits
    return pl.pallas_call(waiting, in_specs=specs, **options)(*arrays, *after)


def channel_body(query_rows, key_rows, value_rows, out_grad, filter_rows, skip_gain):
    devices = lax.axis_size(AXES)
    tokens, channels = query_rows.shape
    length = tokens * devices
    factor = 1.0 / math.sqrt(length)
    scale = 1.0 / (2 * length)
    planes = devices + 1
    tables = [jnp.asarray(table) for table in make_tables(devices, tokens)]
    blocks = math.gcd(devices, 8)
    grid = (devices // blocks,)
    back_rows = 2 * tokens + SPARE
    rows_spec = pl.BlockSpec((tokens, blocks * LANES), lambda i: (0, i))
    vector_spec = pl.BlockSpec((1, blocks * LANES), lambda i: (0, i))
    single_spec = pl.BlockSpec((blocks, tokens, LANES), lambda i: (i, 0, 0))
    rows_shape = jax.ShapeDtypeStruct((tokens, channels), BF16)
    single_shape = jax.ShapeDtypeStruct((devices, tokens, LANES), BF16)
    double_shape = jax.ShapeDtypeStruct((devices, 2 * tokens, LANES), BF16)
    back_shape = jax.ShapeDtypeStruct((devices, back_rows, LANES), BF16)
    narrow = pltpu.VMEM((planes, 2 * tokens, LANES), F32)
    wide = pltpu.VMEM((planes, 2 * tokens, 2 * LANES), F32)

    in_hbm = pl.BlockSpec(memory_space=pltpu.HBM)
    groups = math.gcd(devices, GROUPS)
    packed = kernel(
        pack_kernel, filter_rows, key_rows, value_rows, in_specs=[in_hbm] * 3, out_specs=in_hbm,
        out_shape=double_shape, compiler_params=limit(56),
        scratch_shapes=[
            pltpu.VMEM((3, tokens, channels), BF16), pltpu.VMEM((devices, 2 * tokens, LANES), BF16),
            pltpu.SemaphoreType.DMA((3, groups)), pltpu.SemaphoreType.DMA((groups,)),
        ],
    )
    gate = kernel(
        gate_kernel, query_rows, out_grad, after=[packed], grid=grid,
        in_specs=[rows_spec] * 2, out_specs=single_spec, out_shape=single_shape,
    )
    packed = exchange(packed)
    gate = exchange(gate)
    convolved, spectra = kernel(
        functools.partial(forward_kernel, scale), packed, *tables,
        out_shape=[single_shape, jax.ShapeDtypeStruct((planes, 2 * tokens, 2 * LANES), F32)],
        scratch_shapes=[wide, narrow], compiler_params=limit(48),
    )
    convolved = exchange(convolved)
    back = kernel(
        functools.partial(backward_kernel, scale, factor), gate, packed, spectra, *tables,
        out_shape=back_shape, scratch_shapes=[narrow, narrow, wide], compiler_params=limit(52),
    )
    back = exchange(back)
    whole = pl.BlockSpec(memory_space=pltpu.VMEM)
    branches = (query_rows, out_grad, key_rows, value_rows)
    gain = skip_gain[None, :]
    layer_out, query_grad = kernel(
        mixing_kernel, convolved, *branches, gain, grid=grid, in_specs=[whole] + [rows_spec] * 4 + [vector_spec],
        out_specs=[rows_spec] * 2, out_shape=[rows_shape] * 2, compiler_params=limit(24),
    )
    key_grad, value_grad, filter_grad, skip_grad = kernel(
        carried_kernel, back, *branches, gain, in_specs=[in_hbm] + [whole] * 5,
        out_specs=[in_hbm] * 3 + [pl.BlockSpec()],
        out_shape=[rows_shape] * 3 + [jax.ShapeDtypeStruct((1, channels), F32)], compiler_params=limit(24),
        scratch_shapes=[
            pltpu.VMEM((devices, back_rows, LANES), BF16), pltpu.VMEM((3, tokens, channels), BF16),
            pltpu.SemaphoreType.DMA((groups,)), pltpu.SemaphoreType.DMA((3, groups)),
        ],
    )
    return (layer_out, query_grad, key_grad, value_grad, filter_grad, skip_grad[0])


def rounded_trig(phase, modulus):
    angle = (phase % modulus).astype(jnp.float32) * (TWO_PI / modulus)
    return (jnp.cos(angle).astype(jnp.bfloat16), jnp.sin(angle).astype(jnp.bfloat16))


def regroup_blocks(blocks):
    return lax.all_to_all(blocks, ("outer", "inner"), split_axis=0, concat_axis=0, tiled=True)


def frequency_body(query_rows, key_rows, value_rows, out_grad, filter_rows, skip_gain):
    devices = lax.axis_size(("outer", "inner"))
    position = lax.axis_index(("outer", "inner"))
    tokens_here = query_rows.shape[0]
    channels = query_rows.shape[1]
    piece_rows = tokens_here // devices
    length = tokens_here * devices
    points = 2 * length
    radix_count = 2 * devices
    factor = 1.0 / math.sqrt(length)
    product = (key_rows.astype(jnp.float32) * value_rows.astype(jnp.float32)).astype(jnp.bfloat16)
    gate_grad = out_grad.astype(jnp.float32) * query_rows.astype(jnp.float32)
    signals = jnp.stack([product, gate_grad.astype(jnp.bfloat16), filter_rows], axis=1)
    columns = regroup_blocks(signals.reshape(devices, piece_rows, 3, channels))
    anchor = jnp.arange(devices, dtype=jnp.int32)
    halves = jnp.arange(2, dtype=jnp.int32)
    local_steps = jnp.arange(piece_rows, dtype=jnp.int32)
    step_index = jnp.arange(tokens_here, dtype=jnp.int32)
    sample = position * piece_rows + local_steps
    section_one = []
    for half in range(2):
        freq_one = half * devices + anchor
        phase = (
            anchor[None, None, :] * freq_one[None, :, None] * tokens_here
            + sample[:, None, None] * freq_one[None, :, None]
        )
        one_cos, one_sin = rounded_trig(phase, points)
        table_one = jnp.stack([one_cos, -one_sin], axis=2).reshape(piece_rows, 2 * devices, devices)
        result = jnp.einsum(
            "skr,rsbc->ksbc", table_one, columns, preferred_element_type=jnp.float32
        )
        section_one.append(result.astype(jnp.bfloat16).reshape(devices, 2, piece_rows, 3, channels))
    section_one = regroup_blocks(jnp.stack(section_one, axis=2))
    full_sample = anchor[:, None] * piece_rows + local_steps[None, :]
    step_cos, step_sin = rounded_trig(
        full_sample[:, :, None] * step_index[None, None, :], tokens_here
    )
    real_col = jnp.stack([step_cos, step_sin])
    imag_col = jnp.stack([-step_sin, step_cos])
    table_two = jnp.stack([real_col, imag_col], axis=3)
    section_three = []
    for half in range(2):
        spectra = jnp.einsum(
            "oisbc,iosjk->jkbc",
            section_one[:, :, half],
            table_two,
            preferred_element_type=jnp.float32,
        )
        spec_real, spec_imag = (spectra[0], spectra[1])
        value_real, gate_real, filter_real = (spec_real[:, 0], spec_real[:, 1], spec_real[:, 2])
        value_imag, gate_imag, filter_imag = (spec_imag[:, 0], spec_imag[:, 1], spec_imag[:, 2])
        forward_real = value_real * filter_real - value_imag * filter_imag
        forward_imag = value_real * filter_imag + value_imag * filter_real
        backward_real = filter_real * gate_real + filter_imag * gate_imag
        backward_imag = filter_real * gate_imag - filter_imag * gate_real
        lag_real = (value_real * gate_real + value_imag * gate_imag) * factor
        lag_imag = (value_real * gate_imag - value_imag * gate_real) * factor
        products = jnp.stack(
            [
                jnp.stack([forward_real, backward_real, lag_real], axis=1),
                jnp.stack([forward_imag, backward_imag, lag_imag], axis=1),
            ]
        ).astype(jnp.bfloat16)
        freq_held = half * devices + position
        phase_three = (
            step_index[None, :] * step_index[:, None] * radix_count
            + step_index[None, :] * freq_held
        )
        three_cos, three_sin = rounded_trig(phase_three, points)
        real_row = jnp.stack([three_cos, -three_sin])
        imag_row = jnp.stack([three_sin, three_cos])
        table_three = jnp.stack([real_row, imag_row], axis=2)
        result = jnp.einsum(
            "ikbc,ikjs->sjbc", products, table_three, preferred_element_type=jnp.float32
        )
        section_three.append(result.astype(jnp.bfloat16))
    section_three = jnp.stack(section_three, axis=2).reshape(devices, piece_rows, 2, 2, 3, channels)
    rows_back = regroup_blocks(section_three)
    freq_last = halves[:, None] * devices + anchor[None, :]
    last_cos, last_sin = rounded_trig(anchor[None, None, :] * freq_last[:, :, None], radix_count)
    table_four = jnp.stack([last_cos, -last_sin])
    restored = (
        jnp.einsum("opjhbc,jhor->rpbc", rows_back, table_four, preferred_element_type=jnp.float32)
        / points
    )
    home_rows = regroup_blocks(restored.astype(jnp.bfloat16)).reshape(tokens_here, 3, channels)
    convolved = home_rows[:, 0].astype(jnp.float32)
    correlated = home_rows[:, 1].astype(jnp.float32)
    filter_grad = home_rows[:, 2]
    product_full = product.astype(jnp.float32)
    mixing = convolved + skip_gain[None, :] * product_full
    layer_out = (query_rows.astype(jnp.float32) * mixing).astype(jnp.bfloat16)
    query_grad = (out_grad.astype(jnp.float32) * mixing).astype(jnp.bfloat16)
    carried = correlated + skip_gain[None, :] * gate_grad
    key_grad = (carried * value_rows.astype(jnp.float32)).astype(jnp.bfloat16)
    value_grad = (carried * key_rows.astype(jnp.float32)).astype(jnp.bfloat16)
    skip_part = jnp.sum(gate_grad * product_full, axis=0)
    skip_sum = lax.psum(skip_part, ("outer", "inner"))
    return (layer_out, query_grad, key_grad, value_grad, filter_grad, skip_sum * factor)


def body(*arrays):
    lanes_full = arrays[0].shape[1] == lax.axis_size(AXES) * LANES
    return (channel_body if lanes_full else frequency_body)(*arrays)


def solution(mesh):
    return jax.shard_map(
        body,
        mesh=mesh,
        in_specs=(
            P(("outer", "inner"), None),
            P(("outer", "inner"), None),
            P(("outer", "inner"), None),
            P(("outer", "inner"), None),
            P(("outer", "inner"), None),
            P(),
        ),
        out_specs=(
            P(("outer", "inner"), None),
            P(("outer", "inner"), None),
            P(("outer", "inner"), None),
            P(("outer", "inner"), None),
            P(("outer", "inner"), None),
            P(),
        ),
        check_vma=False,
    )
```

```python
import functools
import math

import jax
import jax.numpy as jnp
import ml_dtypes
import numpy as np
from jax import lax
from jax.experimental import pallas as pl
from jax.experimental.pallas import tpu as pltpu
from jax.sharding import PartitionSpec as P

TWO_PI = 2.0 * math.pi
AXES = ("outer", "inner")
LANES = 128
SUBLANES = 8
GROUPS = 4
SPARE = SUBLANES
BF16 = jnp.bfloat16
F32 = jnp.float32


def table_trig(phase, modulus):
    angle = (phase % modulus).astype(np.float32) * np.float32(TWO_PI / modulus)
    return tuple(
        part.astype(ml_dtypes.bfloat16).astype(np.float32) for part in (np.cos(angle), np.sin(angle))
    )


def make_tables(rows, steps):
    planes = rows + 1
    points = 2 * rows * steps
    row = np.arange(rows)
    plane = np.arange(planes)
    step = np.arange(steps)
    eye = np.eye(SUBLANES, dtype=np.float32)
    phase = row[None, None, :] * plane[None, :, None] * steps + step[:, None, None] * plane[None, :, None]
    cos, sin = table_trig(phase, points)
    first = np.stack([cos, -sin], axis=1).reshape(steps // SUBLANES, SUBLANES, 2, planes, rows)
    first = np.einsum("bipkr,ij->bpkirj", first, eye)
    first = first.reshape(steps // SUBLANES, 2 * planes * SUBLANES, rows * SUBLANES)
    cos, sin = table_trig(step[:, None] * step[None, :], steps)
    second = np.block([[cos, sin], [-sin, cos]])
    phase = step[None, :, None] * step[None, None, :] * (2 * rows) + step[None, :, None] * plane[:, None, None]
    cos, sin = table_trig(phase, points)
    third = np.concatenate(
        [np.concatenate([cos, -sin], axis=2), np.concatenate([sin, cos], axis=2)], axis=1
    )
    cos, sin = table_trig(row[:, None] * plane[None, :], 2 * rows)
    weight = np.where((plane == 0) | (plane == rows), 1.0, 2.0).astype(np.float32)
    last = np.stack([cos * weight, -sin * weight], axis=1)
    last = np.einsum("rpk,ij->ripkj", last, eye).reshape(rows * SUBLANES, 2 * planes * SUBLANES)
    return tuple(table.astype(ml_dtypes.bfloat16) for table in (first, second, third, last))


def dot(a, b):
    return jnp.dot(a, b, preferred_element_type=F32)


def product_of(key, value):
    return (key.astype(F32) * value.astype(F32)).astype(BF16)


def row_group(b, size=2 * SUBLANES):
    return pl.ds(pl.multiple_of(b * size, size), size)


def pack_kernel(filter_ref, key_ref, value_ref, out_ref, held, made, arrived, left):
    tokens, groups = filter_ref.shape[0], arrived.shape[1]
    blocks = out_ref.shape[0] // groups
    sources = (filter_ref, key_ref, value_ref)

    def copies_in(g):
        cols = pl.ds(g * blocks * LANES, blocks * LANES)
        return [pltpu.make_async_copy(ref.at[:, cols], held.at[i, :, cols], arrived.at[i, g]) for i, ref in enumerate(sources)]

    def copy_out(g):
        some = pl.ds(g * blocks, blocks)
        return pltpu.make_async_copy(made.at[some], out_ref.at[some], left.at[g])

    for g in range(groups):
        for copy in copies_in(g):
            copy.start()
    for g in range(groups):
        for copy in copies_in(g):
            copy.wait()
        for d in range(g * blocks, (g + 1) * blocks):
            cols = pl.ds(d * LANES, LANES)
            made[d, :tokens, :] = held[0, :, cols]
            made[d, tokens:, :] = product_of(held[1, :, cols], held[2, :, cols])
        copy_out(g).start()
    for g in range(groups):
        copy_out(g).wait()


def gate_kernel(query_ref, grad_ref, out_ref):
    for d in range(out_ref.shape[0]):
        cols = pl.ds(d * LANES, LANES)
        out_ref[d] = (grad_ref[:, cols].astype(F32) * query_ref[:, cols].astype(F32)).astype(BF16)


def looped(count, chunk, one):
    def several(i, _):
        for j in range(chunk):
            one(i * chunk + j)
        return 0

    lax.fori_loop(0, count // chunk, several, 0)
    for i in range(count - count % chunk, count):
        one(i)


def spectrum_of(read, first_ref, second_ref, section, store):
    planes, steps, width = section.shape[0], section.shape[1] // 2, section.shape[2]

    def one(b):
        pair = read(b)
        for half in range(2):
            block = pair[:, half * SUBLANES : (half + 1) * SUBLANES, :]
            result = dot(first_ref[2 * b + half], block.reshape(-1, width).astype(BF16))
            result = result.reshape(2, planes, SUBLANES, width)
            section[:, row_group(2 * b + half, SUBLANES), :] = result[0]
            section[:, row_group(2 * b + half + steps // SUBLANES, SUBLANES), :] = result[1]

    looped(steps // (2 * SUBLANES), 2, one)

    def two(k):
        store(k, dot(second_ref[...], section[k].astype(BF16)))

    looped(planes, 8, two)


def inverse_of(product_at, third_ref, last_ref, section, scale, write):
    planes, steps, width = section.shape[0], section.shape[1] // 2, section.shape[2]

    def three(k):
        section[k] = dot(third_ref[k], product_at(k))

    looped(planes, 8, three)

    def four(b):
        halves = []
        for half in range(2):
            real = section[:, row_group(2 * b + half, SUBLANES), :].reshape(-1, width)
            imag = section[:, row_group(2 * b + half + steps // SUBLANES, SUBLANES), :].reshape(-1, width)
            flat = jnp.concatenate([real, imag], axis=0).astype(BF16)
            halves.append((dot(last_ref[...], flat) * scale).reshape(-1, SUBLANES, width))
        write(b, jnp.concatenate(halves, axis=1).astype(BF16))

    looped(steps // (2 * SUBLANES), 2, four)


def parts_of(plane):
    steps = plane.shape[0] // 2
    return plane[:steps], plane[steps:]


def conj_product(a, b):
    (ar, ai), (br, bi) = parts_of(a), parts_of(b)
    return jnp.concatenate([ar * br + ai * bi, ar * bi - ai * br], axis=0)


def forward_kernel(scale, packed_ref, first_ref, second_ref, third_ref, last_ref, out_ref, spectra_ref, wide, narrow):
    pairs = packed_ref.shape[1] // (4 * SUBLANES)

    def read(b):
        filt, value = packed_ref[:, row_group(b), :], packed_ref[:, row_group(b + pairs), :]
        return jnp.concatenate([filt.astype(F32), value.astype(F32)], axis=2)

    def store(k, plane):
        spectra_ref[k] = plane

    spectrum_of(read, first_ref, second_ref, wide, store)

    def product_at(k):
        (fr, fi), (vr, vi) = parts_of(spectra_ref[k, :, :LANES]), parts_of(spectra_ref[k, :, LANES:])
        return jnp.concatenate([vr * fr - vi * fi, vr * fi + vi * fr], axis=0).astype(BF16)

    def write(b, rows):
        out_ref[:, row_group(b), :] = rows

    inverse_of(product_at, third_ref, last_ref, narrow, scale, write)


def split_rows(total):
    rows = []
    for _ in range(3):
        rows.append(total.astype(BF16).astype(F32))
        total = total - rows[-1]
    rows.append(jnp.zeros((SPARE - len(rows), total.shape[1]), F32))
    return jnp.concatenate(rows, axis=0).astype(BF16)


def backward_kernel(scale, factor, gate_ref, packed_ref, spectra_ref, first_ref, second_ref, third_ref, last_ref, out_ref, section, gate_spectrum, wide):
    steps = gate_ref.shape[1]
    pairs = steps // (2 * SUBLANES)

    def gate_times_product(d, total):
        return total + gate_ref[d].astype(F32) * packed_ref[d, steps:, :].astype(F32)

    total = lax.fori_loop(0, gate_ref.shape[0], gate_times_product, jnp.zeros((steps, LANES), F32))
    spare = split_rows(jnp.sum(total, axis=0, keepdims=True) * factor)
    for d in range(out_ref.shape[0]):
        out_ref[d, 2 * steps :, :] = spare

    def read(b):
        return gate_ref[:, row_group(b), :].astype(F32)

    def store(k, plane):
        gate_spectrum[k] = plane

    spectrum_of(read, first_ref, second_ref, section, store)

    def product_at(k):
        gate = gate_spectrum[k]
        back = conj_product(spectra_ref[k, :, :LANES], gate)
        lag = conj_product(spectra_ref[k, :, LANES:], gate) * factor
        return jnp.concatenate([back, lag], axis=1).astype(BF16)

    def write(b, rows):
        out_ref[:, row_group(b), :] = rows[:, :, :LANES]
        out_ref[:, row_group(b + pairs), :] = rows[:, :, LANES:]

    inverse_of(product_at, third_ref, last_ref, wide, scale, write)


def mixing_kernel(conv_ref, query_ref, grad_ref, key_ref, value_ref, gain_ref, layer_ref, query_grad_ref):
    blocks = layer_ref.shape[1] // LANES
    for d in range(blocks):
        cols = pl.ds(d * LANES, LANES)
        query, grad, gain = query_ref[:, cols].astype(F32), grad_ref[:, cols].astype(F32), gain_ref[:, cols]
        product = product_of(key_ref[:, cols], value_ref[:, cols]).astype(F32)
        mixing = conv_ref[pl.program_id(0) * blocks + d].astype(F32) + gain * product
        layer_ref[:, cols] = (query * mixing).astype(BF16)
        query_grad_ref[:, cols] = (grad * mixing).astype(BF16)


def carried_kernel(back_ref, query_ref, grad_ref, key_ref, value_ref, gain_ref, *refs):
    *row_refs, skip_ref, back, made, arrived, left = refs
    tokens, groups = key_ref.shape[0], arrived.shape[0]
    blocks = back_ref.shape[0] // groups

    def copy_in(g):
        some = pl.ds(g * blocks, blocks)
        return pltpu.make_async_copy(back_ref.at[some], back.at[some], arrived.at[g])

    def copies_out(g):
        cols = pl.ds(g * blocks * LANES, blocks * LANES)
        return [pltpu.make_async_copy(made.at[i, :, cols], ref.at[:, cols], left.at[i, g]) for i, ref in enumerate(row_refs)]

    for g in range(groups):
        copy_in(g).start()
    for g in range(groups):
        copy_in(g).wait()
        for d in range(g * blocks, (g + 1) * blocks):
            cols = pl.ds(d * LANES, LANES)
            gate = grad_ref[:, cols].astype(F32) * query_ref[:, cols].astype(F32)
            carried = back[d, :tokens, :].astype(F32) + gain_ref[:, cols] * gate
            made[0, :, cols] = (carried * value_ref[:, cols].astype(F32)).astype(BF16)
            made[1, :, cols] = (carried * key_ref[:, cols].astype(F32)).astype(BF16)
            made[2, :, cols] = back[d, tokens : 2 * tokens, :]
            skip_ref[:, cols] = jnp.sum(back[d, 2 * tokens :, :].astype(F32), axis=0, keepdims=True)
        for copy in copies_out(g):
            copy.start()
    for g in range(groups):
        for copy in copies_out(g):
            copy.wait()


def exchange(blocks):
    return lax.all_to_all(blocks, AXES, split_axis=0, concat_axis=0, tiled=True)


def limit(mib):
    return pltpu.CompilerParams(vmem_limit_bytes=mib * 1024 * 1024)


def kernel(body, *arrays, after=(), in_specs=None, **options):
    count, waits = len(arrays), len(after)

    def waiting(*refs):
        body(*refs[:count], *refs[count + waits :])

    specs = list(in_specs or [pl.BlockSpec()] * count) + [pl.BlockSpec(memory_space=pl.ANY)] * waits
    return pl.pallas_call(waiting, in_specs=specs, **options)(*arrays, *after)


def channel_body(query_rows, key_rows, value_rows, out_grad, filter_rows, skip_gain):
    devices = lax.axis_size(AXES)
    tokens, channels = query_rows.shape
    length = tokens * devices
    factor = 1.0 / math.sqrt(length)
    scale = 1.0 / (2 * length)
    planes = devices + 1
    tables = [jnp.asarray(table) for table in make_tables(devices, tokens)]
    blocks = math.gcd(devices, 8)
    grid = (devices // blocks,)
    back_rows = 2 * tokens + SPARE
    rows_spec = pl.BlockSpec((tokens, blocks * LANES), lambda i: (0, i))
    vector_spec = pl.BlockSpec((1, blocks * LANES), lambda i: (0, i))
    single_spec = pl.BlockSpec((blocks, tokens, LANES), lambda i: (i, 0, 0))
    rows_shape = jax.ShapeDtypeStruct((tokens, channels), BF16)
    single_shape = jax.ShapeDtypeStruct((devices, tokens, LANES), BF16)
    double_shape = jax.ShapeDtypeStruct((devices, 2 * tokens, LANES), BF16)
    back_shape = jax.ShapeDtypeStruct((devices, back_rows, LANES), BF16)
    narrow = pltpu.VMEM((planes, 2 * tokens, LANES), F32)
    wide = pltpu.VMEM((planes, 2 * tokens, 2 * LANES), F32)

    in_hbm = pl.BlockSpec(memory_space=pltpu.HBM)
    groups = math.gcd(devices, GROUPS)
    packed = kernel(
        pack_kernel, filter_rows, key_rows, value_rows, in_specs=[in_hbm] * 3, out_specs=in_hbm,
        out_shape=double_shape, compiler_params=limit(56),
        scratch_shapes=[
            pltpu.VMEM((3, tokens, channels), BF16), pltpu.VMEM((devices, 2 * tokens, LANES), BF16),
            pltpu.SemaphoreType.DMA((3, groups)), pltpu.SemaphoreType.DMA((groups,)),
        ],
    )
    gate = kernel(
        gate_kernel, query_rows, out_grad, after=[packed], grid=grid,
        in_specs=[rows_spec] * 2, out_specs=single_spec, out_shape=single_shape,
    )
    packed = exchange(packed)
    gate = exchange(gate)
    convolved, spectra = kernel(
        functools.partial(forward_kernel, scale), packed, *tables,
        out_shape=[single_shape, jax.ShapeDtypeStruct((planes, 2 * tokens, 2 * LANES), F32)],
        scratch_shapes=[wide, narrow], compiler_params=limit(48),
    )
    convolved = exchange(convolved)
    back = kernel(
        functools.partial(backward_kernel, scale, factor), gate, packed, spectra, *tables,
        out_shape=back_shape, scratch_shapes=[narrow, narrow, wide], compiler_params=limit(52),
    )
    back = exchange(back)
    whole = pl.BlockSpec(memory_space=pltpu.VMEM)
    branches = (query_rows, out_grad, key_rows, value_rows)
    gain = skip_gain[None, :]
    layer_out, query_grad = kernel(
        mixing_kernel, convolved, *branches, gain, grid=grid, in_specs=[whole] + [rows_spec] * 4 + [vector_spec],
        out_specs=[rows_spec] * 2, out_shape=[rows_shape] * 2, compiler_params=limit(24),
    )
    key_grad, value_grad, filter_grad, skip_grad = kernel(
        carried_kernel, back, *branches, gain, in_specs=[in_hbm] + [whole] * 5,
        out_specs=[in_hbm] * 3 + [pl.BlockSpec()],
        out_shape=[rows_shape] * 3 + [jax.ShapeDtypeStruct((1, channels), F32)], compiler_params=limit(24),
        scratch_shapes=[
            pltpu.VMEM((devices, back_rows, LANES), BF16), pltpu.VMEM((3, tokens, channels), BF16),
            pltpu.SemaphoreType.DMA((groups,)), pltpu.SemaphoreType.DMA((3, groups)),
        ],
    )
    return (layer_out, query_grad, key_grad, value_grad, filter_grad, skip_grad[0])


def rounded_trig(phase, modulus):
    angle = (phase % modulus).astype(jnp.float32) * (TWO_PI / modulus)
    return (jnp.cos(angle).astype(jnp.bfloat16), jnp.sin(angle).astype(jnp.bfloat16))


def regroup_blocks(blocks):
    return lax.all_to_all(blocks, ("outer", "inner"), split_axis=0, concat_axis=0, tiled=True)


def frequency_body(query_rows, key_rows, value_rows, out_grad, filter_rows, skip_gain):
    devices = lax.axis_size(("outer", "inner"))
    position = lax.axis_index(("outer", "inner"))
    tokens_here = query_rows.shape[0]
    channels = query_rows.shape[1]
    piece_rows = tokens_here // devices
    length = tokens_here * devices
    points = 2 * length
    radix_count = 2 * devices
    factor = 1.0 / math.sqrt(length)
    product = (key_rows.astype(jnp.float32) * value_rows.astype(jnp.float32)).astype(jnp.bfloat16)
    gate_grad = out_grad.astype(jnp.float32) * query_rows.astype(jnp.float32)
    signals = jnp.stack([product, gate_grad.astype(jnp.bfloat16), filter_rows], axis=1)
    columns = regroup_blocks(signals.reshape(devices, piece_rows, 3, channels))
    anchor = jnp.arange(devices, dtype=jnp.int32)
    halves = jnp.arange(2, dtype=jnp.int32)
    local_steps = jnp.arange(piece_rows, dtype=jnp.int32)
    step_index = jnp.arange(tokens_here, dtype=jnp.int32)
    sample = position * piece_rows + local_steps
    section_one = []
    for half in range(2):
        freq_one = half * devices + anchor
        phase = (
            anchor[None, None, :] * freq_one[None, :, None] * tokens_here
            + sample[:, None, None] * freq_one[None, :, None]
        )
        one_cos, one_sin = rounded_trig(phase, points)
        table_one = jnp.stack([one_cos, -one_sin], axis=2).reshape(piece_rows, 2 * devices, devices)
        result = jnp.einsum(
            "skr,rsbc->ksbc", table_one, columns, preferred_element_type=jnp.float32
        )
        section_one.append(result.astype(jnp.bfloat16).reshape(devices, 2, piece_rows, 3, channels))
    section_one = regroup_blocks(jnp.stack(section_one, axis=2))
    full_sample = anchor[:, None] * piece_rows + local_steps[None, :]
    step_cos, step_sin = rounded_trig(
        full_sample[:, :, None] * step_index[None, None, :], tokens_here
    )
    real_col = jnp.stack([step_cos, step_sin])
    imag_col = jnp.stack([-step_sin, step_cos])
    table_two = jnp.stack([real_col, imag_col], axis=3)
    section_three = []
    for half in range(2):
        spectra = jnp.einsum(
            "oisbc,iosjk->jkbc",
            section_one[:, :, half],
            table_two,
            preferred_element_type=jnp.float32,
        )
        spec_real, spec_imag = (spectra[0], spectra[1])
        value_real, gate_real, filter_real = (spec_real[:, 0], spec_real[:, 1], spec_real[:, 2])
        value_imag, gate_imag, filter_imag = (spec_imag[:, 0], spec_imag[:, 1], spec_imag[:, 2])
        forward_real = value_real * filter_real - value_imag * filter_imag
        forward_imag = value_real * filter_imag + value_imag * filter_real
        backward_real = filter_real * gate_real + filter_imag * gate_imag
        backward_imag = filter_real * gate_imag - filter_imag * gate_real
        lag_real = (value_real * gate_real + value_imag * gate_imag) * factor
        lag_imag = (value_real * gate_imag - value_imag * gate_real) * factor
        products = jnp.stack(
            [
                jnp.stack([forward_real, backward_real, lag_real], axis=1),
                jnp.stack([forward_imag, backward_imag, lag_imag], axis=1),
            ]
        ).astype(jnp.bfloat16)
        freq_held = half * devices + position
        phase_three = (
            step_index[None, :] * step_index[:, None] * radix_count
            + step_index[None, :] * freq_held
        )
        three_cos, three_sin = rounded_trig(phase_three, points)
        real_row = jnp.stack([three_cos, -three_sin])
        imag_row = jnp.stack([three_sin, three_cos])
        table_three = jnp.stack([real_row, imag_row], axis=2)
        result = jnp.einsum(
            "ikbc,ikjs->sjbc", products, table_three, preferred_element_type=jnp.float32
        )
        section_three.append(result.astype(jnp.bfloat16))
    section_three = jnp.stack(section_three, axis=2).reshape(devices, piece_rows, 2, 2, 3, channels)
    rows_back = regroup_blocks(section_three)
    freq_last = halves[:, None] * devices + anchor[None, :]
    last_cos, last_sin = rounded_trig(anchor[None, None, :] * freq_last[:, :, None], radix_count)
    table_four = jnp.stack([last_cos, -last_sin])
    restored = (
        jnp.einsum("opjhbc,jhor->rpbc", rows_back, table_four, preferred_element_type=jnp.float32)
        / points
    )
    home_rows = regroup_blocks(restored.astype(jnp.bfloat16)).reshape(tokens_here, 3, channels)
    convolved = home_rows[:, 0].astype(jnp.float32)
    correlated = home_rows[:, 1].astype(jnp.float32)
    filter_grad = home_rows[:, 2]
    product_full = product.astype(jnp.float32)
    mixing = convolved + skip_gain[None, :] * product_full
    layer_out = (query_rows.astype(jnp.float32) * mixing).astype(jnp.bfloat16)
    query_grad = (out_grad.astype(jnp.float32) * mixing).astype(jnp.bfloat16)
    carried = correlated + skip_gain[None, :] * gate_grad
    key_grad = (carried * value_rows.astype(jnp.float32)).astype(jnp.bfloat16)
    value_grad = (carried * key_rows.astype(jnp.float32)).astype(jnp.bfloat16)
    skip_part = jnp.sum(gate_grad * product_full, axis=0)
    skip_sum = lax.psum(skip_part, ("outer", "inner"))
    return (layer_out, query_grad, key_grad, value_grad, filter_grad, skip_sum * factor)


def body(*arrays):
    lanes_full = arrays[0].shape[1] == lax.axis_size(AXES) * LANES
    return (channel_body if lanes_full else frequency_body)(*arrays)


def solution(mesh):
    return jax.shard_map(
        body,
        mesh=mesh,
        in_specs=(
            P(("outer", "inner"), None),
            P(("outer", "inner"), None),
            P(("outer", "inner"), None),
            P(("outer", "inner"), None),
            P(("outer", "inner"), None),
            P(),
        ),
        out_specs=(
            P(("outer", "inner"), None),
            P(("outer", "inner"), None),
            P(("outer", "inner"), None),
            P(("outer", "inner"), None),
            P(("outer", "inner"), None),
            P(),
        ),
        check_vma=False,
    )
```
